256 devices in a mesh: ctx: 32 (over x_hi, z, core), head: 8 (over x_lo, y).
Axes of the slice: x: 4 (x_hi: 2, x_lo: 2; x = x_hi * 2 + x_lo), y: 4, z: 8, core: 2. Of those that a mesh axis runs over, the one named last changes fastest.
Arguments:
- queries: bfloat16 [5120, 3072], P('ctx', 'head'), may hold values from -10 to 10
- keys: bfloat16 [5120, 3072], P('ctx', 'head'), may hold values from -6 to 6
- values: bfloat16 [5120, 3072], P('ctx', 'head'), may hold values from -6 to 6
- tan_queries: bfloat16 [5120, 3072], P('ctx', 'head'), may hold values from -6 to 6
- tan_keys: bfloat16 [5120, 3072], P('ctx', 'head'), may hold values from -6 to 6
- tan_values: bfloat16 [5120, 3072], P('ctx', 'head'), may hold values from -6 to 6
- w_out: bfloat16 [3072, 3072], P('head'), may hold values from -0.15625 to 0.15625
Outputs:
- projected: bfloat16 [5120, 3072], P('ctx', 'head')
- projected_tangent: bfloat16 [5120, 3072], P('ctx', 'head')
The draws below stay inside these ranges and needn't reach their ends.
All inputs are finite; a program needn't handle non-finite values.
Results may differ from the reference program's by a relative error of at most 0.02.
Values may be sent and summed in bfloat16 or wider, within the bound.
No kernel may reach another device: no remote copies, remote signals or barrier semaphores. Data moves between devices by JAX's collectives and lax.ppermute only.
A program may use at most 64 MiB of HBM per device.

```python
import math
import jax
import jax.numpy as jnp
from jax import lax

HEADS = 24
DH = 128
D = 3072
SEQ = 5120
N_HEAD = 8


def draw_queries(key, part):
    key = jax.random.fold_in(key, 11)
    base = 2.5 * jax.random.truncated_normal(key, -4.0, 4.0, (SEQ, D), jnp.float32)
    return base.astype(jnp.bfloat16)


def draw_keys(key, part):
    key = jax.random.fold_in(key, 12)
    base = jax.random.truncated_normal(key, -6.0, 6.0, (SEQ, D), jnp.float32)
    return base.astype(jnp.bfloat16)


def raised(values, key, source, target, parts, factor):
    def block_of(position):
        return (jnp.arange(values.shape[position]) // (values.shape[position] // parts)).reshape((-1,) + (1,) * (values.ndim - 1 - position))

    near = jax.random.permutation(key, parts)[block_of(target)]
    other_side = (block_of(target) + parts // 2) % parts
    return jnp.where((block_of(source) == near) | (block_of(source) == other_side), factor * values, values)


def shard_levels(rng, shape, pieces, low, largest):
    loudness, own = 1.0, jax.random.fold_in(rng, 6)
    for axis_at, blocks in pieces:
        draws = jnp.exp(jax.random.uniform(jax.random.fold_in(own, axis_at), (blocks,), jnp.float32, low / len(pieces), largest / len(pieces)))
        loudness = loudness * jnp.repeat(draws, shape[axis_at] // blocks).reshape([-1 if axis == axis_at else 1 for axis in range(len(shape))])
    return loudness


def normal_values(rng, extent, deviation, most, cuts=(), kind=jnp.bfloat16):
    gain = shard_levels(rng, extent, cuts, -0.22, 0.18) if cuts else 1.0
    result = jax.random.normal(rng, extent, jnp.float32) * deviation * gain
    return jnp.minimum(jnp.maximum(result, -most), most).astype(kind)


def noise_with(rng, shape, width, reach, shards, heavy, kind=jnp.bfloat16):
    drawn = width * jax.random.normal(rng, shape, jnp.float32)
    if shards:
        drawn = drawn * shard_levels(rng, shape, shards, -0.22, 0.18)
    return jnp.clip(raised(drawn, jax.random.fold_in(rng, 3), *heavy), -reach, reach).astype(kind)


def setup_inputs(seed: int = 0) -> dict:
    streams_of = jax.random.split(jax.random.key(seed), 8)
    queries = draw_queries(jax.random.fold_in(streams_of[7], 71), 0)
    keys = draw_keys(jax.random.fold_in(streams_of[7], 71), 0)
    values = normal_values(streams_of[2], (SEQ, D), 1.0, 6.0, ((0, 32), (1, 8)))
    tan_queries = normal_values(streams_of[3], (SEQ, D), 1.0, 6.0, ((0, 32), (1, 8)))
    tan_keys = normal_values(streams_of[4], (SEQ, D), 1.0, 6.0, ((0, 32), (1, 8)))
    tan_values = normal_values(streams_of[5], (SEQ, D), 1.0, 6.0, ((0, 32), (1, 8)))
    w_out = noise_with(streams_of[6], (D, D), D ** -0.5, 0.15625, ((0, 8),), (0, 1, 8, 2.0))
    return {"queries": queries, "keys": keys, "values": values, "tan_queries": tan_queries, "tan_keys": tan_keys, "tan_values": tan_values, "w_out": w_out}


def by_heads(matrix):
    return matrix.reshape(matrix.shape[0], HEADS, DH).transpose(1, 0, 2)

def attend_block(query_block, tangent_block, key_heads, value_heads, tan_key_heads, tan_value_heads):
    factor = 1.0 / math.sqrt(DH)
    scores = jnp.dot(query_block, key_heads.T, preferred_element_type=jnp.float32) * factor
    slopes = (jnp.dot(tangent_block, key_heads.T, preferred_element_type=jnp.float32) + jnp.dot(query_block, tan_key_heads.T, preferred_element_type=jnp.float32)) * factor
    row_peak = lax.optimization_barrier(jnp.max(scores, axis=1, keepdims=True))
    weights = jnp.exp(scores - row_peak)
    mixed_terms = weights * slopes
    row_total = lax.optimization_barrier(jnp.sum(weights, axis=1, keepdims=True))
    slope_total = lax.optimization_barrier(jnp.sum(mixed_terms, axis=1, keepdims=True))
    weights_low = weights.astype(jnp.bfloat16)
    mixed_low = mixed_terms.astype(jnp.bfloat16)
    primal_sum = jnp.dot(weights_low, value_heads, preferred_element_type=jnp.float32)
    tangent_sum = jnp.dot(weights_low, tan_value_heads, preferred_element_type=jnp.float32) + jnp.dot(mixed_low, value_heads, preferred_element_type=jnp.float32)
    attended = primal_sum / row_total
    tangent_out = tangent_sum / row_total - slope_total / row_total * attended
    return (attended.astype(jnp.bfloat16), tangent_out.astype(jnp.bfloat16))

def grouped_projection(matrix, w_out):
    group_width = D // N_HEAD
    column_groups = matrix.reshape(SEQ, N_HEAD, group_width).transpose(1, 0, 2)
    weight_groups = w_out.reshape(N_HEAD, group_width, D)

    def add_group(total, paired):
        part_value = jnp.dot(paired[0], paired[1], preferred_element_type=jnp.float32).astype(jnp.bfloat16)
        part_value = lax.optimization_barrier(part_value)
        return (total + part_value.astype(jnp.float32), None)
    total, unused = lax.scan(add_group, jnp.zeros((SEQ, D), jnp.float32), (column_groups, weight_groups))
    return total.astype(jnp.bfloat16)

def reference(queries, keys, values, tan_queries, tan_keys, tan_values, w_out):
    block_rows = 512 if SEQ % 512 == 0 else SEQ
    block_count = SEQ // block_rows

    def one_head(inputs):
        query_heads, tangent_heads, key_heads, value_heads, tan_key_heads, tan_value_heads = inputs
        query_blocks = query_heads.reshape(block_count, block_rows, DH)
        tangent_blocks = tangent_heads.reshape(block_count, block_rows, DH)

        def one_block(paired):
            return attend_block(paired[0], paired[1], key_heads, value_heads, tan_key_heads, tan_value_heads)
        attended, tangent_out = lax.map(one_block, (query_blocks, tangent_blocks))
        return (attended.reshape(SEQ, DH), tangent_out.reshape(SEQ, DH))
    members = tuple((by_heads(member) for member in (queries, tan_queries, keys, values, tan_keys, tan_values)))
    attended, tangent_out = lax.map(one_head, members)
    attended = attended.transpose(1, 0, 2).reshape(SEQ, D)
    tangent_out = tangent_out.transpose(1, 0, 2).reshape(SEQ, D)
    projected = grouped_projection(attended, w_out)
    projected_tangent = grouped_projection(tangent_out, w_out)
    return (projected, projected_tangent)
```

```python
import math

import jax
import jax.numpy as jnp
from jax import lax
from jax.experimental import pallas as pl
from jax.experimental.pallas import tpu as pltpu
from jax.sharding import Mesh, PartitionSpec as P

DH = 128
FACTOR = 1.0 / math.sqrt(DH)
LOG2E = math.log2(math.e)
CTX = (("xh", 2), ("z", 8), ("core", 2))
HEAD = (("xl", 2), ("y", 4))
GROUPS = 8
VMEM_LIMIT = 48 * 1024 * 1024
PARAMS = pltpu.CompilerParams(vmem_limit_bytes=VMEM_LIMIT)

_NT = (((1,), (1,)), ((), ()))


def vmem():
    return pl.BlockSpec(memory_space=pltpu.VMEM)


def call(kernel, name, outs, args, flops=0, transcendentals=0):
    moved = sum(x.size * x.dtype.itemsize for x in list(args) + list(outs))
    return pl.pallas_call(
        kernel,
        in_specs=[vmem()] * len(args),
        out_specs=[vmem()] * len(outs),
        out_shape=list(outs),
        compiler_params=PARAMS,
        cost_estimate=pl.CostEstimate(
            flops=flops, bytes_accessed=moved, transcendentals=transcendentals
        ),
        name=name,
    )(*args)


def shape(rows, columns, dtype=jnp.bfloat16):
    return jax.ShapeDtypeStruct((rows, columns), dtype)


def with_stats(rows, logs, slopes, split):
    lane = lax.broadcasted_iota(jnp.int32, (rows, DH), 1)
    stats = jnp.zeros((rows, DH), jnp.float32)
    at = 0
    for column in logs + slopes:
        for _ in range(3 if split else 1):
            part = column.astype(jnp.bfloat16).astype(jnp.float32) if split else column
            stats = jnp.where(lane == at, part, stats)
            column = column - part
            at += 1
    return stats


def stats_of(part, heads):
    split = 3 if part.dtype == jnp.bfloat16 else 1
    stats = part[:, 2 * heads * DH :].astype(jnp.float32)
    columns = [
        sum(stats[:, at * split + i : at * split + i + 1] for i in range(split))
        for at in range(2 * heads)
    ]
    return columns[:heads], columns[heads:]


def joined(parts, logs, slopes):
    top = logs[0]
    for log in logs[1:]:
        top = jnp.maximum(top, log)
    shares = [jnp.exp(log - top) for log in logs]
    total = sum(shares)
    inverse = 1.0 / total
    shares = [share * inverse for share in shares]
    mean_slope = sum(share * slope for share, slope in zip(shares, slopes))
    primal = sum(share * part[0] for share, part in zip(shares, parts))
    tangent = sum(
        share * part[1] + (share * (slope - mean_slope)) * part[0]
        for share, slope, part in zip(shares, slopes, parts)
    )
    return primal, tangent, top + jnp.log(total), mean_slope


def head_of(part, head):
    both = part[:, 2 * head * DH : 2 * (head + 1) * DH].astype(jnp.float32)
    return both[:, :DH], both[:, DH:]


def attend_head(q_both, k_both, v_both):
    s = lax.dot_general(q_both[:, DH:], k_both[:, :DH], _NT, preferred_element_type=jnp.float32)
    slope = lax.dot_general(q_both, k_both, _NT, preferred_element_type=jnp.float32)
    peak = jnp.max(s, axis=1, keepdims=True)
    weights = jnp.exp2((s - peak) * (FACTOR * LOG2E))
    mixed = weights * slope
    total = jnp.sum(weights, axis=1, keepdims=True)
    slope_total = jnp.sum(mixed, axis=1, keepdims=True)
    sums = jnp.dot(weights.astype(jnp.bfloat16), v_both, preferred_element_type=jnp.float32)
    more = jnp.dot(mixed.astype(jnp.bfloat16), v_both[:, :DH], preferred_element_type=jnp.float32)
    inverse = 1.0 / total
    mean_slope = slope_total * inverse * FACTOR
    primal = sums[:, :DH] * inverse
    tangent = (sums[:, DH:] + more * FACTOR) * inverse - mean_slope * primal
    return primal, tangent, peak * FACTOR + jnp.log(total), mean_slope


def attend_kernel(q_count, k_count, merge, *refs):
    q_refs, k_refs = refs[:q_count], refs[q_count : q_count + k_count]
    earlier = refs[q_count + k_count : 2 * q_count + k_count] if merge else ()
    outs = refs[-q_count:]
    rows, heads = q_refs[0].shape[0], q_refs[0].shape[1] // (2 * DH)
    logs, slopes = [[] for _ in outs], [[] for _ in outs]
    for head in range(heads):
        k_all = jnp.concatenate(
            [ref[:, 4 * head * DH : 4 * (head + 1) * DH] for ref in k_refs], axis=0
        )
        for pair in range(0, q_count, 2):
            q_both = jnp.concatenate(
                [ref[:, 2 * head * DH : 2 * (head + 1) * DH] for ref in q_refs[pair : pair + 2]],
                axis=0,
            )
            found = attend_head(q_both, k_all[:, : 2 * DH], k_all[:, 2 * DH :])
            for half in range(2):
                at = pair + half
                primal, tangent, log, slope = (x[half * rows : (half + 1) * rows] for x in found)
                if merge:
                    old = earlier[at][...]
                    old_logs, old_slopes = stats_of(old, heads)
                    primal, tangent, log, slope = joined(
                        [(primal, tangent), head_of(old, head)],
                        [log, old_logs[head]],
                        [slope, old_slopes[head]],
                    )
                first = 2 * head * DH
                outs[at][:, first : first + DH] = primal.astype(outs[at].dtype)
                outs[at][:, first + DH : first + 2 * DH] = tangent.astype(outs[at].dtype)
                logs[at].append(log)
                slopes[at].append(slope)
    for at, out in enumerate(outs):
        stats = with_stats(rows, logs[at], slopes[at], merge)
        out[:, 2 * heads * DH :] = stats.astype(out.dtype)


def attend(q_blocks, k_blocks, earlier=None):
    rows, width = q_blocks[0].shape
    keys = sum(block.shape[0] for block in k_blocks)
    merge = earlier is not None
    outs = [shape(rows, width + DH, jnp.bfloat16 if merge else jnp.float32)] * len(q_blocks)
    pairs = len(q_blocks) * rows * keys * (width // (2 * DH))

    def kernel(*refs):
        attend_kernel(len(q_blocks), len(k_blocks), merge, *refs)

    return call(
        kernel,
        "attend",
        outs,
        list(q_blocks) + list(k_blocks) + list(earlier or ()),
        flops=2 * pairs * DH * 8,
        transcendentals=pairs,
    )


def join_kernel(a_ref, b_ref, out):
    parts = [a_ref[...], b_ref[...]]
    rows = out.shape[0]
    heads = (out.shape[1] - DH) // (2 * DH)
    stats = [stats_of(part, heads) for part in parts]
    logs, slopes = [], []
    for head in range(heads):
        primal, tangent, log, slope = joined(
            [head_of(part, head) for part in parts],
            [stat[0][head] for stat in stats],
            [stat[1][head] for stat in stats],
        )
        first = 2 * head * DH
        out[:, first : first + DH] = primal.astype(out.dtype)
        out[:, first + DH : first + 2 * DH] = tangent.astype(out.dtype)
        logs.append(log)
        slopes.append(slope)
    out[:, 2 * heads * DH :] = with_stats(rows, logs, slopes, True).astype(out.dtype)


def project_kernel(a_ref, b_ref, c_ref, w_ref, out):
    parts = [ref[...] for ref in (a_ref, b_ref, c_ref)]
    heads = (a_ref.shape[1] - DH) // (2 * DH)
    stats = [stats_of(part, heads) for part in parts]
    found = [
        joined(
            [head_of(part, head) for part in parts],
            [stat[0][head] for stat in stats],
            [stat[1][head] for stat in stats],
        )
        for head in range(heads)
    ]
    attended = jnp.concatenate(
        [
            jnp.concatenate([f[at].astype(jnp.bfloat16) for f in found], axis=1)
            for at in range(2)
        ],
        axis=0,
    )
    columns = out.shape[2]
    for group in range(out.shape[0]):
        out[group] = jnp.dot(
            attended,
            w_ref[:, group * columns : (group + 1) * columns],
            preferred_element_type=jnp.float32,
        ).astype(out.dtype)


def total_kernel(parts_ref, value_ref, tangent_ref):
    total = parts_ref[0].astype(jnp.float32)
    for group in range(1, parts_ref.shape[0]):
        total = total + parts_ref[group].astype(jnp.float32)
    rows = value_ref.shape[0]
    value_ref[...] = total[:rows].astype(value_ref.dtype)
    tangent_ref[...] = total[rows:].astype(tangent_ref.dtype)


def pack_kernel(count, *refs):
    out = refs[count]
    for at, ref in enumerate(refs[:count]):
        for head in range(ref.shape[1] // DH):
            to = (head * count + at) * DH
            out[:, to : to + DH] = ref[:, head * DH : (head + 1) * DH]


def pack(*arrays):
    def kernel(*refs):
        pack_kernel(len(arrays), *refs)

    rows, width = arrays[0].shape
    return call(kernel, "pack", [shape(rows, width * len(arrays))], arrays)[0]


SWAP = [(0, 1), (1, 0)]


def along_z(x, step):
    return lax.ppermute(x, "z", [(i, (i + step) % 8) for i in range(8)])


def on_device(queries, keys, values, tan_queries, tan_keys, tan_values, w_out):
    rows, width = queries.shape
    packed = pack(keys, tan_keys, values, tan_values)
    up, down = [along_z(packed, 1)], [along_z(packed, -1)]

    own_q = pack(tan_queries, queries)
    far_q = lax.ppermute(own_q, "xh", SWAP)
    near_q = [own_q, lax.ppermute(own_q, "core", SWAP)]
    away_q = [far_q, lax.ppermute(far_q, "core", SWAP)]

    for _ in range(2):
        up.append(along_z(up[-1], 1))
        down.append(along_z(down[-1], -1))
    half = rows // 2
    last = [along_z(up[2][:half], 1), along_z(down[2][half:], -1)]

    first_keys = [packed, up[0], down[0], up[1]]
    last_keys = [down[1], up[2], down[2]] + last
    states = attend(near_q + away_q, first_keys)
    away, away_other = attend(away_q, last_keys, states[2:])
    away_parts = [away, lax.ppermute(away_other, "core", SWAP)]
    near, near_other = attend(near_q, last_keys, states[:2])
    to_far = call(join_kernel, "join", [shape(*away.shape)], away_parts)[0]
    parts = call(
        project_kernel,
        "project",
        [jax.ShapeDtypeStruct((GROUPS, 2 * rows, w_out.shape[1] // GROUPS), jnp.bfloat16)],
        [
            near,
            lax.ppermute(near_other, "core", SWAP),
            lax.ppermute(to_far, "xh", SWAP),
            w_out,
        ],
        flops=4 * rows * w_out.shape[0] * w_out.shape[1],
    )[0]
    parts = lax.all_to_all(parts, ("xl", "y"), 0, 0)
    return tuple(call(total_kernel, "total", [shape(rows, width)] * 2, [parts]))


def solution(mesh):
    fine = Mesh(
        mesh.devices.reshape([size for _, size in CTX + HEAD]), [name for name, _ in CTX + HEAD]
    )
    ctx, head = tuple(name for name, _ in CTX), tuple(name for name, _ in HEAD)
    split = P(ctx, head)
    return jax.shard_map(
        on_device,
        mesh=fine,
        in_specs=(split,) * 6 + (P(head, None),),
        out_specs=(split, split),
        check_vma=False,
    )
```

```python
import math

import jax
import jax.numpy as jnp
from jax import lax
from jax.experimental import pallas as pl
from jax.experimental.pallas import tpu as pltpu
from jax.sharding import Mesh, PartitionSpec as P

DH = 128
FACTOR = 1.0 / math.sqrt(DH)
LOG2E = math.log2(math.e)
CTX = (("xh", 2), ("z", 8), ("core", 2))
HEAD = (("xl", 2), ("y", 4))
GROUPS = 8
VMEM_LIMIT = 20 * 1024 * 1024
PARAMS = pltpu.CompilerParams(vmem_limit_bytes=VMEM_LIMIT)

_NT = (((1,), (1,)), ((), ()))


def vmem():
    return pl.BlockSpec(memory_space=pltpu.VMEM)


def call(kernel, name, outs, args, flops=0, transcendentals=0, moves=True):
    moved = sum(x.size * x.dtype.itemsize for x in list(args) + list(outs)) if moves else 0
    return pl.pallas_call(
        kernel,
        in_specs=[vmem()] * len(args),
        out_specs=[vmem()] * len(outs),
        out_shape=list(outs),
        compiler_params=PARAMS,
        cost_estimate=pl.CostEstimate(
            flops=flops, bytes_accessed=moved, transcendentals=transcendentals
        ),
        name=name,
    )(*args)


def shape(rows, columns, dtype=jnp.bfloat16):
    return jax.ShapeDtypeStruct((rows, columns), dtype)


def wide(column):
    return jnp.broadcast_to(column, (column.shape[0], DH))


def tiled(x, columns):
    whole = -(-columns // DH)
    return jnp.concatenate([x] * whole, axis=1)[:, :columns]


def stats_columns(logs, slopes):
    rows = logs[0].shape[0]
    lane = lax.broadcasted_iota(jnp.int32, (rows, DH), 1)
    stats = jnp.zeros((rows, DH), jnp.float32)
    at = 0
    for value in logs + slopes:
        for _ in range(3):
            part = value.astype(jnp.bfloat16).astype(jnp.float32)
            stats = jnp.where(lane == at, part, stats)
            value = value - part
            at += 1
    return stats.astype(jnp.bfloat16)


def stats_of(part, heads):
    row = lax.broadcasted_iota(jnp.int32, (DH, 2 * heads * DH), 0)
    column = lax.broadcasted_iota(jnp.int32, (DH, 2 * heads * DH), 1)
    first = 3 * lax.shift_right_logical(column, DH.bit_length() - 1)
    chosen = ((row >= first) & (row < first + 3)).astype(jnp.bfloat16)
    sums = jnp.dot(part[:, 2 * heads * DH :], chosen, preferred_element_type=jnp.float32)
    columns = [sums[:, at * DH : (at + 1) * DH] for at in range(2 * heads)]
    return columns[:heads], columns[heads:]


def joined(parts, logs, slopes):
    top = logs[0]
    for log in logs[1:]:
        top = jnp.maximum(top, log)
    shares = [jnp.exp(log - top) for log in logs]
    total = sum(shares)
    inverse = 1.0 / total
    shares = [share * inverse for share in shares]
    mean_slope = sum(share * slope for share, slope in zip(shares, slopes))
    primal = sum(share * part[0] for share, part in zip(shares, parts))
    tangent = sum(
        share * (part[1] + (slope - mean_slope) * part[0])
        for share, slope, part in zip(shares, slopes, parts)
    )
    return primal, tangent, top + jnp.log(total), mean_slope


def head_of(part, head):
    both = part[:, 2 * head * DH : 2 * (head + 1) * DH].astype(jnp.float32)
    return both[:, :DH], both[:, DH:]


def attend_head(q_both, k_both, v_both, state):
    s = lax.dot_general(q_both[:, DH:], k_both[:, :DH], _NT, preferred_element_type=jnp.float32)
    slope = lax.dot_general(q_both, k_both, _NT, preferred_element_type=jnp.float32)
    peak = wide(jnp.max(s, axis=1, keepdims=True))
    if state is not None:
        peak = jnp.maximum(peak, state[2])
    weights = jnp.exp2((s - tiled(peak, s.shape[1])) * (FACTOR * LOG2E))
    total = wide(jnp.sum(weights, axis=1, keepdims=True))
    mixed = (weights * slope).astype(jnp.bfloat16)
    sums = jnp.dot(weights.astype(jnp.bfloat16), v_both, preferred_element_type=jnp.float32)
    value_one = jnp.concatenate([v_both[:, :DH], jnp.ones_like(v_both[:, :DH])], axis=1)
    more = jnp.dot(mixed, value_one, preferred_element_type=jnp.float32) * FACTOR
    primal, tangent, slope_total = sums[:, :DH], sums[:, DH:] + more[:, :DH], more[:, DH:]
    if state is not None:
        shrink = jnp.exp2((state[2] - peak) * (FACTOR * LOG2E))
        primal = primal + state[0] * shrink
        tangent = tangent + state[1] * shrink
        total = total + state[3] * shrink
        slope_total = slope_total + state[4] * shrink
    return primal, tangent, peak, total, slope_total


def attend_kernel(q_count, k_count, merge, final, *refs):
    q_refs, k_refs = refs[:q_count], refs[q_count : q_count + k_count]
    earlier = refs[q_count + k_count : 2 * q_count + k_count] if merge else ()
    outs = refs[-q_count:]
    rows, heads = q_refs[0].shape[0], q_refs[0].shape[1] // (2 * DH)
    logs, slopes = [[] for _ in outs], [[] for _ in outs]

    def both(some, head):
        halves = [
            jnp.concatenate([ref[:, at * DH : (at + 1) * DH] for ref in some], axis=0)
            for at in (head, heads + head)
        ]
        return jnp.concatenate(halves, axis=1)

    for head in range(heads):
        k_both, v_both = both(k_refs[0::2], head), both(k_refs[1::2], head)
        for pair in range(0, q_count, 2):
            q_both = both(q_refs[pair : pair + 2], head)
            state = None
            if merge:
                state = [
                    jnp.concatenate(
                        [
                            ref[:, (5 * head + at) * DH : (5 * head + at + 1) * DH]
                            for ref in earlier[pair : pair + 2]
                        ],
                        axis=0,
                    )
                    for at in range(5)
                ]
            found = attend_head(q_both, k_both, v_both, state)
            for half in range(2):
                out = outs[pair + half]
                own = [x[half * rows : (half + 1) * rows] for x in found]
                if final:
                    primal, tangent, peak, total, slope_total = own
                    inverse = 1.0 / total
                    mean_slope = slope_total * inverse
                    primal = primal * inverse
                    tangent = tangent * inverse - mean_slope * primal
                    first = 2 * head * DH
                    out[:, first : first + DH] = primal.astype(out.dtype)
                    out[:, first + DH : first + 2 * DH] = tangent.astype(out.dtype)
                    logs[pair + half].append(peak * FACTOR + jnp.log(total))
                    slopes[pair + half].append(mean_slope)
                else:
                    for at, x in enumerate(own):
                        out[:, (5 * head + at) * DH : (5 * head + at + 1) * DH] = x
    if final:
        for at, out in enumerate(outs):
            out[:, 2 * heads * DH :] = stats_columns(logs[at], slopes[at])


def attend(q_blocks, k_blocks, earlier=None, final=False, hurried=True):
    rows, width = q_blocks[0].shape
    heads = width // (2 * DH)
    keys = sum(block.shape[0] for block in k_blocks) // 2
    merge = earlier is not None
    if final:
        outs = [shape(rows, (2 * heads + 1) * DH)] * len(q_blocks)
    else:
        outs = [shape(rows, 5 * heads * DH, jnp.float32)] * len(q_blocks)
    pairs = len(q_blocks) * rows * keys * heads

    def kernel(*refs):
        attend_kernel(len(q_blocks), len(k_blocks), merge, final, *refs)

    return call(
        kernel,
        "attend",
        outs,
        list(q_blocks) + list(k_blocks) + list(earlier or ()),
        flops=2 * pairs * DH * 8 if hurried else 0,
        transcendentals=pairs if hurried else 0,
        moves=hurried,
    )


def join_parts(refs):
    parts = [ref[...] for ref in refs]
    heads = (parts[0].shape[1] - DH) // (2 * DH)
    stats = [stats_of(part, heads) for part in parts]
    return [
        joined(
            [head_of(part, head) for part in parts],
            [stat[0][head] for stat in stats],
            [stat[1][head] for stat in stats],
        )
        for head in range(heads)
    ]


def join_kernel(a_ref, b_ref, out):
    found = join_parts((a_ref, b_ref))
    for head, (primal, tangent, _, _) in enumerate(found):
        first = 2 * head * DH
        out[:, first : first + DH] = primal.astype(out.dtype)
        out[:, first + DH : first + 2 * DH] = tangent.astype(out.dtype)
    out[:, 2 * len(found) * DH :] = stats_columns([f[2] for f in found], [f[3] for f in found])


def project_kernel(a_ref, b_ref, w_ref, out):
    found = join_parts((a_ref, b_ref))
    attended = jnp.concatenate(
        [
            jnp.concatenate([f[at].astype(jnp.bfloat16) for f in found], axis=1)
            for at in range(2)
        ],
        axis=0,
    )
    columns = out.shape[2]
    for group in range(out.shape[0]):
        out[group] = jnp.dot(
            attended,
            w_ref[:, group * columns : (group + 1) * columns],
            preferred_element_type=jnp.float32,
        ).astype(out.dtype)


def total_kernel(parts_ref, value_ref, tangent_ref):
    total = parts_ref[0].astype(jnp.float32)
    for group in range(1, parts_ref.shape[0]):
        total = total + parts_ref[group].astype(jnp.float32)
    rows = value_ref.shape[0]
    value_ref[...] = total[:rows].astype(value_ref.dtype)
    tangent_ref[...] = total[rows:].astype(tangent_ref.dtype)


SWAP = [(0, 1), (1, 0)]


def along_z(x, step):
    return lax.ppermute(x, "z", [(i, (i + step) % 8) for i in range(8)])


def beside(left, right):
    width = left.shape[1]
    low = jnp.array(-jnp.inf, left.dtype)
    return jnp.maximum(
        lax.pad(left, low, [(0, 0, 0), (0, width, 0)]),
        lax.pad(right, low, [(0, 0, 0), (width, 0, 0)]),
    )


def on_device(queries, keys, values, tan_queries, tan_keys, tan_values, w_out):
    rows, width = queries.shape
    own = [beside(keys, tan_keys), beside(values, tan_values)]
    up, down = [own], [own]

    def hand_on():
        up.append([along_z(x, 1) for x in up[-1]])
        down.append([along_z(x, -1) for x in down[-1]])

    hand_on()
    own_q = beside(tan_queries, queries)
    own_q, up[1][0] = lax.optimization_barrier((own_q, up[1][0]))
    far_q = lax.ppermute(own_q, "xh", SWAP)
    near_q = [own_q, lax.ppermute(own_q, "core", SWAP)]
    away_q = [far_q, lax.ppermute(far_q, "core", SWAP)]

    hand_on()
    up.append([along_z(up[2][0], 1)])
    down.append([along_z(down[2][0], -1)])
    states = attend(near_q + away_q, own + up[1] + down[1])
    up[2][1], states = lax.optimization_barrier((up[2][1], states))
    up[3].append(along_z(up[2][1], 1))
    down[3].append(along_z(down[2][1], -1))
    states = attend(near_q + away_q, up[2] + down[2], states)
    up[3][0], states = lax.optimization_barrier((up[3][0], states))
    last = [along_z(up[3][0], 1), along_z(down[3][1], -1)]
    states = attend(near_q + away_q, up[3] + down[3], states)

    away, away_other = attend(away_q, last, states[2:], True)
    whole = [shape(*away.shape)]
    to_far = call(join_kernel, "join", whole, [away, lax.ppermute(away_other, "core", SWAP)])[0]
    to_far, near_states = lax.optimization_barrier((to_far, states[:2]))
    from_far = lax.ppermute(to_far, "xh", SWAP)
    near, near_other = attend(near_q, last, near_states, True, False)
    near_parts = [near, lax.ppermute(near_other, "core", SWAP)]
    near = call(join_kernel, "join", whole, near_parts, moves=False)[0]
    parts = call(
        project_kernel,
        "project",
        [jax.ShapeDtypeStruct((GROUPS, 2 * rows, w_out.shape[1] // GROUPS), jnp.bfloat16)],
        [near, from_far, w_out],
        flops=4 * rows * w_out.shape[0] * w_out.shape[1],
    )[0]
    parts = lax.all_to_all(parts, ("xl", "y"), 0, 0)
    return tuple(call(total_kernel, "total", [shape(rows, width)] * 2, [parts]))


def solution(mesh):
    fine = Mesh(
        mesh.devices.reshape([size for _, size in CTX + HEAD]), [name for name, _ in CTX + HEAD]
    )
    ctx, head = tuple(name for name, _ in CTX), tuple(name for name, _ in HEAD)
    split = P(ctx, head)
    return jax.shard_map(
        on_device,
        mesh=fine,
        in_specs=(split,) * 6 + (P(head, None),),
        out_specs=(split, split),
        check_vma=False,
    )
```

```python
import math

import jax
import jax.numpy as jnp
from jax import lax
from jax.experimental import pallas as pl
from jax.experimental.pallas import tpu as pltpu
from jax.sharding import Mesh, PartitionSpec as P

DH = 128
FACTOR = 1.0 / math.sqrt(DH)
LOG2E = math.log2(math.e)
CTX = (("xh", 2), ("z", 8), ("core", 2))
HEAD = (("xl", 2), ("y", 4))
GROUPS = 8
VMEM_LIMIT = 20 * 1024 * 1024
PARAMS = pltpu.CompilerParams(vmem_limit_bytes=VMEM_LIMIT)

_NT = (((1,), (1,)), ((), ()))


def vmem():
    return pl.BlockSpec(memory_space=pltpu.VMEM)


def call(kernel, name, outs, args, flops=0, transcendentals=0):
    moved = sum(x.size * x.dtype.itemsize for x in list(args) + list(outs))
    return pl.pallas_call(
        kernel,
        in_specs=[vmem()] * len(args),
        out_specs=[vmem()] * len(outs),
        out_shape=list(outs),
        compiler_params=PARAMS,
        cost_estimate=pl.CostEstimate(
            flops=flops, bytes_accessed=moved, transcendentals=transcendentals
        ),
        name=name,
    )(*args)


def shape(rows, columns, dtype=jnp.bfloat16):
    return jax.ShapeDtypeStruct((rows, columns), dtype)


def wide(column):
    return jnp.broadcast_to(column, (column.shape[0], DH))


def tiled(x, columns):
    whole = -(-columns // DH)
    return jnp.concatenate([x] * whole, axis=1)[:, :columns]


def stats_columns(logs, slopes):
    lane = lax.broadcasted_iota(jnp.int32, logs[0].shape, 1)
    stats = jnp.zeros(logs[0].shape, jnp.float32)
    third = jnp.zeros(logs[0].shape, jnp.int32)
    for at, value in enumerate(logs + slopes):
        stats = jnp.where(lane >= 3 * at, value, stats)
        third = jnp.where(lane >= 3 * at, 3 * at, third)
    third = lane - third
    high = stats.astype(jnp.bfloat16).astype(jnp.float32)
    rest = stats - high
    middle = rest.astype(jnp.bfloat16).astype(jnp.float32)
    kept = jnp.where(third == 0, high, jnp.where(third == 1, middle, rest - middle))
    return jnp.where(third < 3, kept, 0.0).astype(jnp.bfloat16)


def stats_of(part, heads):
    row = lax.broadcasted_iota(jnp.int32, (DH, 2 * heads * DH), 0)
    column = lax.broadcasted_iota(jnp.int32, (DH, 2 * heads * DH), 1)
    first = 3 * lax.shift_right_logical(column, DH.bit_length() - 1)
    chosen = ((row >= first) & (row < first + 3)).astype(jnp.bfloat16)
    sums = jnp.dot(part[:, 2 * heads * DH :], chosen, preferred_element_type=jnp.float32)
    columns = [sums[:, at * DH : (at + 1) * DH] for at in range(2 * heads)]
    return columns[:heads], columns[heads:]


def joined(parts, logs, slopes):
    top = logs[0]
    for log in logs[1:]:
        top = jnp.maximum(top, log)
    shares = [jnp.exp(log - top) for log in logs]
    total = sum(shares)
    inverse = 1.0 / total
    shares = [share * inverse for share in shares]
    mean_slope = sum(share * slope for share, slope in zip(shares, slopes))
    primal = sum(share * part[0] for share, part in zip(shares, parts))
    tangent = sum(
        share * (part[1] + (slope - mean_slope) * part[0])
        for share, slope, part in zip(shares, slopes, parts)
    )
    return primal, tangent, top + jnp.log(total), mean_slope


def head_of(part, head):
    both = part[:, 2 * head * DH : 2 * (head + 1) * DH].astype(jnp.float32)
    return both[:, :DH], both[:, DH:]


def attend_head(q_both, k_both, v_both, state):
    s = lax.dot_general(q_both[:, DH:], k_both[:, :DH], _NT, preferred_element_type=jnp.float32)
    slope = lax.dot_general(q_both, k_both, _NT, preferred_element_type=jnp.float32)
    peak = wide(jnp.max(s, axis=1, keepdims=True))
    if state is not None:
        peak = jnp.maximum(peak, state[2])
    weights = jnp.exp2((s - tiled(peak, s.shape[1])) * (FACTOR * LOG2E))
    total = wide(jnp.sum(weights, axis=1, keepdims=True))
    mixed = (weights * slope).astype(jnp.bfloat16)
    sums = jnp.dot(weights.astype(jnp.bfloat16), v_both, preferred_element_type=jnp.float32)
    value_one = jnp.concatenate([v_both[:, :DH], jnp.ones_like(v_both[:, :DH])], axis=1)
    more = jnp.dot(mixed, value_one, preferred_element_type=jnp.float32) * FACTOR
    primal, tangent, slope_total = sums[:, :DH], sums[:, DH:] + more[:, :DH], more[:, DH:]
    if state is not None:
        shrink = jnp.exp2((state[2] - peak) * (FACTOR * LOG2E))
        primal = primal + state[0] * shrink
        tangent = tangent + state[1] * shrink
        total = total + state[3] * shrink
        slope_total = slope_total + state[4] * shrink
    return primal, tangent, peak, total, slope_total


def attend_kernel(q_count, k_count, merge, final, *refs):
    q_refs, k_refs = refs[:q_count], refs[q_count : q_count + k_count]
    earlier = refs[q_count + k_count : 2 * q_count + k_count] if merge else ()
    outs = refs[-q_count:]
    heads = q_refs[0].shape[1] // (2 * DH)
    logs, slopes = [[] for _ in outs], [[] for _ in outs]

    def both(some, head):
        halves = [
            jnp.concatenate([ref[:, at * DH : (at + 1) * DH] for ref in some], axis=0)
            for at in (head, heads + head)
        ]
        return jnp.concatenate(halves, axis=1)

    for head in range(heads):
        k_both, v_both = both(k_refs[0::2], head), both(k_refs[1::2], head)
        for stack, out in enumerate(outs):
            state = None
            if merge:
                state = [
                    earlier[stack][:, (5 * head + at) * DH : (5 * head + at + 1) * DH]
                    for at in range(5)
                ]
            found = attend_head(both(q_refs[stack : stack + 1], head), k_both, v_both, state)
            if final:
                primal, tangent, peak, total, slope_total = found
                inverse = 1.0 / total
                mean_slope = slope_total * inverse
                primal = primal * inverse
                tangent = tangent * inverse - mean_slope * primal
                first = 2 * head * DH
                out[:, first : first + DH] = primal.astype(out.dtype)
                out[:, first + DH : first + 2 * DH] = tangent.astype(out.dtype)
                logs[stack].append(peak * FACTOR + jnp.log(total))
                slopes[stack].append(mean_slope)
            else:
                for at, x in enumerate(found):
                    out[:, (5 * head + at) * DH : (5 * head + at + 1) * DH] = x
    if final:
        for stack, out in enumerate(outs):
            out[:, 2 * heads * DH :] = stats_columns(logs[stack], slopes[stack])


def attend(q_stacks, k_blocks, earlier=None, final=False):
    rows, width = q_stacks[0].shape
    heads = width // (2 * DH)
    keys = sum(block.shape[0] for block in k_blocks) // 2
    merge = earlier is not None
    if final:
        outs = [shape(rows, (2 * heads + 1) * DH)] * len(q_stacks)
    else:
        outs = [shape(rows, 5 * heads * DH, jnp.float32)] * len(q_stacks)
    pairs = len(q_stacks) * rows * keys * heads

    def kernel(*refs):
        attend_kernel(len(q_stacks), len(k_blocks), merge, final, *refs)

    return call(
        kernel,
        "attend",
        outs,
        list(q_stacks) + list(k_blocks) + list(earlier or ()),
        flops=2 * pairs * DH * 8,
        transcendentals=pairs,
    )


def join_parts(parts):
    heads = (parts[0].shape[1] - DH) // (2 * DH)
    stats = [stats_of(part, heads) for part in parts]
    return [
        joined(
            [head_of(part, head) for part in parts],
            [stat[0][head] for stat in stats],
            [stat[1][head] for stat in stats],
        )
        for head in range(heads)
    ]


def join_kernel(first_row, a_ref, b_ref, out):
    own = pl.ds(first_row, out.shape[0])
    found = join_parts([a_ref[own, :], b_ref[own, :]])
    for head, (primal, tangent, _, _) in enumerate(found):
        first = 2 * head * DH
        out[:, first : first + DH] = primal.astype(out.dtype)
        out[:, first + DH : first + 2 * DH] = tangent.astype(out.dtype)
    out[:, 2 * len(found) * DH :] = stats_columns([f[2] for f in found], [f[3] for f in found])


def project_kernel(a_ref, b_ref, w_ref, out):
    found = join_parts([a_ref[...], b_ref[...]])
    attended = jnp.concatenate(
        [
            jnp.concatenate([f[at].astype(jnp.bfloat16) for f in found], axis=1)
            for at in range(2)
        ],
        axis=0,
    )
    columns = out.shape[2]
    for group in range(out.shape[0]):
        out[group] = jnp.dot(
            attended,
            w_ref[:, group * columns : (group + 1) * columns],
            preferred_element_type=jnp.float32,
        ).astype(out.dtype)


def total_kernel(parts_ref, value_ref, tangent_ref):
    total = parts_ref[0].astype(jnp.float32)
    for group in range(1, parts_ref.shape[0]):
        total = total + parts_ref[group].astype(jnp.float32)
    rows = value_ref.shape[0]
    value_ref[...] = total[:rows].astype(value_ref.dtype)
    tangent_ref[...] = total[rows:].astype(tangent_ref.dtype)


SWAP = [(0, 1), (1, 0)]


def along_z(x, step):
    return lax.ppermute(x, "z", [(i, (i + step) % 8) for i in range(8)])


def beside(left, right):
    width = left.shape[1]
    low = jnp.array(-jnp.inf, left.dtype)
    return jnp.maximum(
        lax.pad(left, low, [(0, 0, 0), (0, width, 0)]),
        lax.pad(right, low, [(0, 0, 0), (width, 0, 0)]),
    )


def on_device(queries, keys, values, tan_queries, tan_keys, tan_values, w_out):
    rows, width = queries.shape
    own = [beside(keys, tan_keys), beside(values, tan_values)]
    def around(pair):
        return along_z(pair[0], 1), along_z(pair[1], -1)

    k_steps, v_steps = [(own[0], own[0])], [(own[1], own[1])]
    k_steps.append(around(k_steps[0]))
    v_steps.append(around(v_steps[0]))

    own_q = beside(tan_queries, queries)
    stack = jnp.concatenate([own_q, lax.ppermute(own_q, "xh", SWAP)], axis=0)
    stacks = [stack, lax.ppermute(stack, "core", SWAP)]

    k_steps.append(around(k_steps[1]))
    v_steps[1], k_steps[1] = lax.optimization_barrier((v_steps[1], k_steps[1]))
    v_steps.append(around(v_steps[1]))
    k_steps[2], v_steps[1] = lax.optimization_barrier((k_steps[2], v_steps[1]))
    k_steps.append(around(k_steps[2]))
    v_steps[2], k_steps[2], stacks = lax.optimization_barrier((v_steps[2], k_steps[2], stacks))
    v_steps.append(around(v_steps[2]))

    def both_ways(step):
        return [x for pair in zip(k_steps[step], v_steps[step]) for x in pair]

    states = attend(stacks, own + both_ways(1))
    k_steps[3], v_steps[2], states = lax.optimization_barrier((k_steps[3], v_steps[2], states))
    last = [along_z(k_steps[3][0], 1)]
    states = attend(stacks, both_ways(2), states)
    v_steps[3], k_steps[3], states = lax.optimization_barrier((v_steps[3], k_steps[3], states))
    last.append(along_z(v_steps[3][1], -1))
    states = attend(stacks, both_ways(3), states)

    other = attend(stacks[1:], last, states[1:], True)[0]
    other = lax.ppermute(other, "core", SWAP)
    mine = attend(stacks[:1], last, states[:1], True)[0]

    def join(first_row):
        def kernel(*refs):
            join_kernel(first_row, *refs)

        return call(kernel, "join", [shape(rows, mine.shape[1])], [mine, other])[0]

    from_far = lax.ppermute(join(rows), "xh", SWAP)
    near = join(0)
    parts = call(
        project_kernel,
        "project",
        [jax.ShapeDtypeStruct((GROUPS, 2 * rows, w_out.shape[1] // GROUPS), jnp.bfloat16)],
        [near, from_far, w_out],
        flops=4 * rows * w_out.shape[0] * w_out.shape[1],
    )[0]
    parts = lax.all_to_all(parts, ("xl", "y"), 0, 0)
    return tuple(call(total_kernel, "total", [shape(rows, width)] * 2, [parts]))


def solution(mesh):
    fine = Mesh(
        mesh.devices.reshape([size for _, size in CTX + HEAD]), [name for name, _ in CTX + HEAD]
    )
    ctx, head = tuple(name for name, _ in CTX), tuple(name for name, _ in HEAD)
    split = P(ctx, head)
    return jax.shard_map(
        on_device,
        mesh=fine,
        in_specs=(split,) * 6 + (P(head, None),),
        out_specs=(split, split),
        check_vma=False,
    )
```

```python
import math

import jax
import jax.numpy as jnp
from jax import lax
from jax.experimental import pallas as pl
from jax.experimental.pallas import tpu as pltpu
from jax.sharding import Mesh, PartitionSpec as P

DH = 128
FACTOR = 1.0 / math.sqrt(DH)
LOG2E = math.log2(math.e)
CTX = (("xh", 2), ("z", 8), ("core", 2))
HEAD = (("xl", 2), ("y", 4))
VMEM_LIMIT = 12 * 1024 * 1024
PARAMS = pltpu.CompilerParams(vmem_limit_bytes=VMEM_LIMIT)

_NT = (((1,), (1,)), ((), ()))


def vmem():
    return pl.BlockSpec(memory_space=pltpu.VMEM)


def call(kernel, name, outs, args, flops=0, transcendentals=0):
    moved = sum(x.size * x.dtype.itemsize for x in list(args) + list(outs))
    return pl.pallas_call(
        kernel,
        in_specs=[vmem()] * len(args),
        out_specs=[vmem()] * len(outs),
        out_shape=list(outs),
        compiler_params=PARAMS,
        cost_estimate=pl.CostEstimate(
            flops=flops, bytes_accessed=moved, transcendentals=transcendentals
        ),
        name=name,
    )(*args)


def shape(rows, columns, dtype=jnp.bfloat16):
    return jax.ShapeDtypeStruct((rows, columns), dtype)


def wide(column):
    return jnp.broadcast_to(column, (column.shape[0], DH))


def tiled(x, columns):
    whole = -(-columns // DH)
    return jnp.concatenate([x] * whole, axis=1)[:, :columns]


def stats_columns(logs, slopes):
    lane = lax.broadcasted_iota(jnp.int32, logs[0].shape, 1)
    stats = jnp.zeros(logs[0].shape, jnp.float32)
    third = jnp.zeros(logs[0].shape, jnp.int32)
    for at, value in enumerate(logs + slopes):
        stats = jnp.where(lane >= 3 * at, value, stats)
        third = jnp.where(lane >= 3 * at, 3 * at, third)
    third = lane - third
    high = stats.astype(jnp.bfloat16).astype(jnp.float32)
    rest = stats - high
    middle = rest.astype(jnp.bfloat16).astype(jnp.float32)
    kept = jnp.where(third == 0, high, jnp.where(third == 1, middle, rest - middle))
    return jnp.where(third < 3, kept, 0.0).astype(jnp.bfloat16)


def stats_of(part, heads):
    row = lax.broadcasted_iota(jnp.int32, (DH, 2 * heads * DH), 0)
    column = lax.broadcasted_iota(jnp.int32, (DH, 2 * heads * DH), 1)
    first = 3 * lax.shift_right_logical(column, DH.bit_length() - 1)
    chosen = ((row >= first) & (row < first + 3)).astype(jnp.bfloat16)
    sums = jnp.dot(part[:, 2 * heads * DH :], chosen, preferred_element_type=jnp.float32)
    columns = [sums[:, at * DH : (at + 1) * DH] for at in range(2 * heads)]
    return columns[:heads], columns[heads:]


def joined(parts, logs, slopes):
    top = logs[0]
    for log in logs[1:]:
        top = jnp.maximum(top, log)
    shares = [jnp.exp(log - top) for log in logs]
    total = sum(shares)
    inverse = 1.0 / total
    shares = [share * inverse for share in shares]
    mean_slope = sum(share * slope for share, slope in zip(shares, slopes))
    primal = sum(share * part[0] for share, part in zip(shares, parts))
    tangent = sum(
        share * (part[1] + (slope - mean_slope) * part[0])
        for share, slope, part in zip(shares, slopes, parts)
    )
    return primal, tangent, top + jnp.log(total), mean_slope


def head_of(part, head):
    both = part[:, 2 * head * DH : 2 * (head + 1) * DH].astype(jnp.float32)
    return both[:, :DH], both[:, DH:]


def attend_head(q_both, k_both, v_both, state):
    s = lax.dot_general(q_both[:, DH:], k_both[:, :DH], _NT, preferred_element_type=jnp.float32)
    slope = lax.dot_general(q_both, k_both, _NT, preferred_element_type=jnp.float32)
    peak = wide(jnp.max(s, axis=1, keepdims=True))
    if state is not None:
        peak = jnp.maximum(peak, state[2])
    weights = jnp.exp2((s - tiled(peak, s.shape[1])) * (FACTOR * LOG2E))
    total = wide(jnp.sum(weights, axis=1, keepdims=True))
    mixed = (weights * slope).astype(jnp.bfloat16)
    sums = jnp.dot(weights.astype(jnp.bfloat16), v_both, preferred_element_type=jnp.float32)
    value_one = jnp.concatenate([v_both[:, :DH], jnp.ones_like(v_both[:, :DH])], axis=1)
    more = jnp.dot(mixed, value_one, preferred_element_type=jnp.float32) * FACTOR
    primal, tangent, slope_total = sums[:, :DH], sums[:, DH:] + more[:, :DH], more[:, DH:]
    if state is not None:
        shrink = jnp.exp2((state[2] - peak) * (FACTOR * LOG2E))
        primal = primal + state[0] * shrink
        tangent = tangent + state[1] * shrink
        total = total + state[3] * shrink
        slope_total = slope_total + state[4] * shrink
    return primal, tangent, peak, total, slope_total


def attend_kernel(q_count, k_count, merge, final, *refs):
    q_refs, k_refs = refs[:q_count], refs[q_count : q_count + k_count]
    earlier = refs[q_count + k_count : 2 * q_count + k_count] if merge else ()
    outs = refs[-q_count:]
    heads = q_refs[0].shape[1] // (2 * DH)
    logs, slopes = [[] for _ in outs], [[] for _ in outs]

    def both(some, head):
        halves = [
            jnp.concatenate([ref[:, at * DH : (at + 1) * DH] for ref in some], axis=0)
            for at in (head, heads + head)
        ]
        return jnp.concatenate(halves, axis=1)

    for head in range(heads):
        k_both, v_both = both(k_refs[0::2], head), both(k_refs[1::2], head)
        for stack, out in enumerate(outs):
            state = None
            if merge:
                state = [
                    earlier[stack][:, (5 * head + at) * DH : (5 * head + at + 1) * DH]
                    for at in range(5)
                ]
            found = attend_head(both(q_refs[stack : stack + 1], head), k_both, v_both, state)
            if final:
                primal, tangent, peak, total, slope_total = found
                inverse = 1.0 / total
                mean_slope = slope_total * inverse
                primal = primal * inverse
                tangent = tangent * inverse - mean_slope * primal
                first = 2 * head * DH
                out[:, first : first + DH] = primal.astype(out.dtype)
                out[:, first + DH : first + 2 * DH] = tangent.astype(out.dtype)
                logs[stack].append(peak * FACTOR + jnp.log(total))
                slopes[stack].append(mean_slope)
            else:
                for at, x in enumerate(found):
                    out[:, (5 * head + at) * DH : (5 * head + at + 1) * DH] = x
    if final:
        for stack, out in enumerate(outs):
            out[:, 2 * heads * DH :] = stats_columns(logs[stack], slopes[stack])


def attend(q_stacks, k_blocks, earlier=None, final=False):
    rows, width = q_stacks[0].shape
    heads = width // (2 * DH)
    keys = sum(block.shape[0] for block in k_blocks) // 2
    merge = earlier is not None
    if final:
        outs = [shape(rows, (2 * heads + 1) * DH)] * len(q_stacks)
    else:
        outs = [shape(rows, 5 * heads * DH, jnp.float32)] * len(q_stacks)
    pairs = len(q_stacks) * rows * keys * heads

    def kernel(*refs):
        attend_kernel(len(q_stacks), len(k_blocks), merge, final, *refs)

    return call(
        kernel,
        "attend",
        outs,
        list(q_stacks) + list(k_blocks) + list(earlier or ()),
        flops=2 * pairs * DH * 8,
        transcendentals=pairs,
    )


def join_parts(parts):
    heads = (parts[0].shape[1] - DH) // (2 * DH)
    stats = [stats_of(part, heads) for part in parts]
    return [
        joined(
            [head_of(part, head) for part in parts],
            [stat[0][head] for stat in stats],
            [stat[1][head] for stat in stats],
        )
        for head in range(heads)
    ]


def join_kernel(first_row, a_ref, b_ref, out):
    own = pl.ds(first_row, out.shape[0])
    found = join_parts([a_ref[own, :], b_ref[own, :]])
    for head, (primal, tangent, _, _) in enumerate(found):
        first = 2 * head * DH
        out[:, first : first + DH] = primal.astype(out.dtype)
        out[:, first + DH : first + 2 * DH] = tangent.astype(out.dtype)
    out[:, 2 * len(found) * DH :] = stats_columns([f[2] for f in found], [f[3] for f in found])


def attended_kernel(a_ref, b_ref, out):
    found = join_parts([a_ref[...], b_ref[...]])
    rows = out.shape[0] // 2
    for head, each in enumerate(found):
        for at in range(2):
            out[at * rows : (at + 1) * rows, head * DH : (head + 1) * DH] = each[at].astype(out.dtype)


def project_kernel(at_ref, own_ref, beside_ref, w_ref, w_mine_ref, w_other_ref, *outs):
    xl, y, core = at_ref[0], at_ref[1], at_ref[2]
    columns = outs[0].shape[1]
    for step, out in enumerate(outs):
        target = lax.rem(y + step, len(outs))
        fetched_by, place = lax.div(target, 2), lax.rem(target, 2)
        first = pl.multiple_of((xl * len(outs) + target) * columns, DH)
        first_beside = pl.ds(pl.multiple_of(place * columns, DH), columns)
        w_beside = jnp.where(
            fetched_by == core, w_mine_ref[:, first_beside], w_other_ref[:, first_beside]
        )
        total = jnp.dot(
            own_ref[...], w_ref[:, pl.ds(first, columns)], preferred_element_type=jnp.float32
        ) + jnp.dot(beside_ref[...], w_beside, preferred_element_type=jnp.float32)
        out[...] = total.astype(out.dtype)


def project(place, own, beside, w_out, w_mine, w_other):
    outs = [shape(*own.shape)] * 4
    return pl.pallas_call(
        project_kernel,
        in_specs=[pl.BlockSpec(memory_space=pltpu.SMEM)] + [vmem()] * 5,
        out_specs=[vmem()] * len(outs),
        out_shape=outs,
        compiler_params=PARAMS,
        name="project",
    )(jnp.stack(place).astype(jnp.int32), own, beside, w_out, w_mine, w_other)


def total_kernel(*refs):
    parts, (value_ref, tangent_ref) = refs[:-2], refs[-2:]
    total = sum(part[...].astype(jnp.float32) for part in parts)
    rows = value_ref.shape[0]
    value_ref[...] = total[:rows].astype(value_ref.dtype)
    tangent_ref[...] = total[rows:].astype(tangent_ref.dtype)


SWAP = [(0, 1), (1, 0)]


def along_z(x, step):
    return lax.ppermute(x, "z", [(i, (i + step) % 8) for i in range(8)])


def beside(left, right):
    width = left.shape[1]
    low = jnp.array(-jnp.inf, left.dtype)
    return jnp.maximum(
        lax.pad(left, low, [(0, 0, 0), (0, width, 0)]),
        lax.pad(right, low, [(0, 0, 0), (width, 0, 0)]),
    )


def on_device(queries, keys, values, tan_queries, tan_keys, tan_values, w_out):
    rows, width = queries.shape
    own = [beside(keys, tan_keys), beside(values, tan_values)]
    def around(pair):
        return along_z(pair[0], 1), along_z(pair[1], -1)

    k_steps, v_steps = [(own[0], own[0])], [(own[1], own[1])]
    k_steps.append(around(k_steps[0]))
    v_steps.append(around(v_steps[0]))

    own_q = beside(tan_queries, queries)
    place = [lax.axis_index(name) for name in ("xl", "y", "core")]
    quarter = w_out.shape[1] // 4
    wanted = lax.dynamic_slice_in_dim(
        w_out, ((1 - place[0]) * 2 + place[2]) * quarter, quarter, axis=1
    )
    far_q = lax.ppermute(own_q, "xh", SWAP)
    wanted, far_q = lax.optimization_barrier((wanted, far_q))
    stack = jnp.concatenate([own_q, far_q], axis=0)
    stacks = [stack, lax.ppermute(stack, "core", SWAP)]

    k_steps.append(around(k_steps[1]))
    v_steps[1], k_steps[1] = lax.optimization_barrier((v_steps[1], k_steps[1]))
    v_steps.append(around(v_steps[1]))
    k_steps[2], v_steps[1] = lax.optimization_barrier((k_steps[2], v_steps[1]))
    k_steps.append(around(k_steps[2]))
    v_steps[2], k_steps[2], stacks = lax.optimization_barrier((v_steps[2], k_steps[2], stacks))
    v_steps.append(around(v_steps[2]))

    wanted, v_steps[1] = lax.optimization_barrier((wanted, v_steps[1]))
    w_mine = lax.ppermute(wanted, "xl", SWAP)

    def both_ways(step):
        return [x for pair in zip(k_steps[step], v_steps[step]) for x in pair]

    states = attend(stacks, own + both_ways(1))
    k_steps[3], v_steps[2], states = lax.optimization_barrier((k_steps[3], v_steps[2], states))
    last = [along_z(k_steps[3][0], 1)]
    states = attend(stacks, both_ways(2), states)
    v_steps[3], k_steps[3], states = lax.optimization_barrier((v_steps[3], k_steps[3], states))
    last.append(along_z(v_steps[3][1], -1))
    states = attend(stacks, both_ways(3), states)

    states, w_mine = lax.optimization_barrier((states, w_mine))
    other = attend(stacks[1:], last, states[1:], True)[0]
    other = lax.ppermute(other, "core", SWAP)
    mine = attend(stacks[:1], last, states[:1], True)[0]

    def join(first_row):
        def kernel(*refs):
            join_kernel(first_row, *refs)

        return call(kernel, "join", [shape(rows, mine.shape[1])], [mine, other])[0]

    from_far = lax.ppermute(join(rows), "xh", SWAP)
    near = join(0)
    attended = call(attended_kernel, "attended", [shape(2 * rows, width)], [near, from_far])[0]
    beside_attended = lax.ppermute(attended, "xl", SWAP)
    w_other = lax.ppermute(w_mine, "core", SWAP)
    parts = list(project(place, attended, beside_attended, w_out, w_mine, w_other))
    parts = parts[:1] + [
        lax.ppermute(part, "y", [(i, (i + step) % 4) for i in range(4)])
        for step, part in enumerate(parts[1:], 1)
    ]
    return tuple(call(total_kernel, "total", [shape(rows, width)] * 2, parts))


def solution(mesh):
    fine = Mesh(
        mesh.devices.reshape([size for _, size in CTX + HEAD]), [name for name, _ in CTX + HEAD]
    )
    ctx, head = tuple(name for name, _ in CTX), tuple(name for name, _ in HEAD)
    split = P(ctx, head)
    return jax.shard_map(
        on_device,
        mesh=fine,
        in_specs=(split,) * 6 + (P(head, None),),
        out_specs=(split, split),
        check_vma=False,
    )
```

```python
import math

import jax
import jax.numpy as jnp
from jax import lax
from jax.experimental import pallas as pl
from jax.experimental.pallas import tpu as pltpu
from jax.sharding import Mesh, PartitionSpec as P

DH = 128
FACTOR = 1.0 / math.sqrt(DH)
LOG2E = math.log2(math.e)
CTX = (("xh", 2), ("z", 8), ("core", 2))
HEAD = (("xl", 2), ("y", 4))
VMEM_LIMIT = 12 * 1024 * 1024
PARAMS = pltpu.CompilerParams(vmem_limit_bytes=VMEM_LIMIT)

_NT = (((1,), (1,)), ((), ()))


def vmem():
    return pl.BlockSpec(memory_space=pltpu.VMEM)


def call(kernel, name, outs, args, flops=0, transcendentals=0):
    moved = sum(x.size * x.dtype.itemsize for x in list(args) + list(outs))
    return pl.pallas_call(
        kernel,
        in_specs=[vmem()] * len(args),
        out_specs=[vmem()] * len(outs),
        out_shape=list(outs),
        compiler_params=PARAMS,
        cost_estimate=pl.CostEstimate(
            flops=flops, bytes_accessed=moved, transcendentals=transcendentals
        ),
        name=name,
    )(*args)


def shape(rows, columns, dtype=jnp.bfloat16):
    return jax.ShapeDtypeStruct((rows, columns), dtype)


def wide(column):
    return jnp.broadcast_to(column, (column.shape[0], DH))


def tiled(x, columns):
    whole = -(-columns // DH)
    return jnp.concatenate([x] * whole, axis=1)[:, :columns]


def stats_columns(logs, slopes):
    lane = lax.broadcasted_iota(jnp.int32, logs[0].shape, 1)
    stats = jnp.zeros(logs[0].shape, jnp.float32)
    third = jnp.zeros(logs[0].shape, jnp.int32)
    for at, value in enumerate(logs + slopes):
        stats = jnp.where(lane >= 3 * at, value, stats)
        third = jnp.where(lane >= 3 * at, 3 * at, third)
    third = lane - third
    high = stats.astype(jnp.bfloat16).astype(jnp.float32)
    rest = stats - high
    middle = rest.astype(jnp.bfloat16).astype(jnp.float32)
    kept = jnp.where(third == 0, high, jnp.where(third == 1, middle, rest - middle))
    return jnp.where(third < 3, kept, 0.0).astype(jnp.bfloat16)


def stats_of(part, heads):
    row = lax.broadcasted_iota(jnp.int32, (DH, 2 * heads * DH), 0)
    column = lax.broadcasted_iota(jnp.int32, (DH, 2 * heads * DH), 1)
    first = 3 * lax.shift_right_logical(column, DH.bit_length() - 1)
    chosen = ((row >= first) & (row < first + 3)).astype(jnp.bfloat16)
    sums = jnp.dot(part[:, 2 * heads * DH :], chosen, preferred_element_type=jnp.float32)
    columns = [sums[:, at * DH : (at + 1) * DH] for at in range(2 * heads)]
    return columns[:heads], columns[heads:]


def joined(parts, logs, slopes):
    top = logs[0]
    for log in logs[1:]:
        top = jnp.maximum(top, log)
    shares = [jnp.exp(log - top) for log in logs]
    total = sum(shares)
    inverse = 1.0 / total
    shares = [share * inverse for share in shares]
    mean_slope = sum(share * slope for share, slope in zip(shares, slopes))
    primal = sum(share * part[0] for share, part in zip(shares, parts))
    tangent = sum(
        share * (part[1] + (slope - mean_slope) * part[0])
        for share, slope, part in zip(shares, slopes, parts)
    )
    return primal, tangent, top + jnp.log(total), mean_slope


def head_of(part, head):
    both = part[:, 2 * head * DH : 2 * (head + 1) * DH].astype(jnp.float32)
    return both[:, :DH], both[:, DH:]


def attend_head(q_both, k_both, v_both, state):
    s = lax.dot_general(q_both[:, DH:], k_both[:, :DH], _NT, preferred_element_type=jnp.float32)
    slope = lax.dot_general(q_both, k_both, _NT, preferred_element_type=jnp.float32)
    peak = wide(jnp.max(s, axis=1, keepdims=True))
    if state is not None:
        peak = jnp.maximum(peak, state[2])
    weights = jnp.exp2((s - tiled(peak, s.shape[1])) * (FACTOR * LOG2E))
    total = wide(jnp.sum(weights, axis=1, keepdims=True))
    mixed = (weights * slope).astype(jnp.bfloat16)
    sums = jnp.dot(weights.astype(jnp.bfloat16), v_both, preferred_element_type=jnp.float32)
    value_one = jnp.concatenate([v_both[:, :DH], jnp.ones_like(v_both[:, :DH])], axis=1)
    more = jnp.dot(mixed, value_one, preferred_element_type=jnp.float32) * FACTOR
    primal, tangent, slope_total = sums[:, :DH], sums[:, DH:] + more[:, :DH], more[:, DH:]
    if state is not None:
        shrink = jnp.exp2((state[2] - peak) * (FACTOR * LOG2E))
        primal = primal + state[0] * shrink
        tangent = tangent + state[1] * shrink
        total = total + state[3] * shrink
        slope_total = slope_total + state[4] * shrink
    return primal, tangent, peak, total, slope_total


def attend_kernel(q_count, k_count, merge, final, *refs):
    q_refs, k_refs = refs[:q_count], refs[q_count : q_count + k_count]
    earlier = refs[q_count + k_count : 2 * q_count + k_count] if merge else ()
    outs = refs[-q_count:]
    heads = q_refs[0].shape[1] // (2 * DH)
    logs, slopes = [[] for _ in outs], [[] for _ in outs]

    def both(some, head):
        halves = [
            jnp.concatenate([ref[:, at * DH : (at + 1) * DH] for ref in some], axis=0)
            for at in (head, heads + head)
        ]
        return jnp.concatenate(halves, axis=1)

    for head in range(heads):
        k_both, v_both = both(k_refs[0::2], head), both(k_refs[1::2], head)
        for stack, out in enumerate(outs):
            state = None
            if merge:
                state = [
                    earlier[stack][:, (5 * head + at) * DH : (5 * head + at + 1) * DH]
                    for at in range(5)
                ]
            found = attend_head(both(q_refs[stack : stack + 1], head), k_both, v_both, state)
            if final:
                primal, tangent, peak, total, slope_total = found
                inverse = 1.0 / total
                mean_slope = slope_total * inverse
                primal = primal * inverse
                tangent = tangent * inverse - mean_slope * primal
                first = 2 * head * DH
                out[:, first : first + DH] = primal.astype(out.dtype)
                out[:, first + DH : first + 2 * DH] = tangent.astype(out.dtype)
                logs[stack].append(peak * FACTOR + jnp.log(total))
                slopes[stack].append(mean_slope)
            else:
                for at, x in enumerate(found):
                    out[:, (5 * head + at) * DH : (5 * head + at + 1) * DH] = x
    if final:
        for stack, out in enumerate(outs):
            out[:, 2 * heads * DH :] = stats_columns(logs[stack], slopes[stack])


def attend(q_stacks, k_blocks, earlier=None, final=False):
    rows, width = q_stacks[0].shape
    heads = width // (2 * DH)
    keys = sum(block.shape[0] for block in k_blocks) // 2
    merge = earlier is not None
    if final:
        outs = [shape(rows, (2 * heads + 1) * DH)] * len(q_stacks)
    else:
        outs = [shape(rows, 5 * heads * DH, jnp.float32)] * len(q_stacks)
    pairs = len(q_stacks) * rows * keys * heads

    def kernel(*refs):
        attend_kernel(len(q_stacks), len(k_blocks), merge, final, *refs)

    return call(
        kernel,
        "attend",
        outs,
        list(q_stacks) + list(k_blocks) + list(earlier or ()),
        flops=2 * pairs * DH * 8,
        transcendentals=pairs,
    )


def join_parts(parts):
    heads = (parts[0].shape[1] - DH) // (2 * DH)
    stats = [stats_of(part, heads) for part in parts]
    return [
        joined(
            [head_of(part, head) for part in parts],
            [stat[0][head] for stat in stats],
            [stat[1][head] for stat in stats],
        )
        for head in range(heads)
    ]


def join_kernel(first_row, a_ref, b_ref, out):
    own = pl.ds(first_row, out.shape[0])
    found = join_parts([a_ref[own, :], b_ref[own, :]])
    for head, (primal, tangent, _, _) in enumerate(found):
        first = 2 * head * DH
        out[:, first : first + DH] = primal.astype(out.dtype)
        out[:, first + DH : first + 2 * DH] = tangent.astype(out.dtype)
    out[:, 2 * len(found) * DH :] = stats_columns([f[2] for f in found], [f[3] for f in found])


def attended_kernel(a_ref, b_ref, out):
    found = join_parts([a_ref[...], b_ref[...]])
    rows = out.shape[0] // 2
    for head, each in enumerate(found):
        for at in range(2):
            out[at * rows : (at + 1) * rows, head * DH : (head + 1) * DH] = each[at].astype(out.dtype)


def project_kernel(at_ref, own_ref, beside_ref, w_ref, w_mine_ref, w_other_ref, *outs):
    xl, y, core = at_ref[0], at_ref[1], at_ref[2]
    columns = outs[0].shape[1]
    both = jnp.concatenate([own_ref[...], beside_ref[...]], axis=1)
    for step, out in enumerate(outs):
        target = lax.rem(y + step, len(outs))
        fetched_by, place = lax.div(target, 2), lax.rem(target, 2)
        first = pl.multiple_of((xl * len(outs) + target) * columns, DH)
        first_beside = pl.ds(pl.multiple_of(place * columns, DH), columns)
        w_beside = jnp.where(
            fetched_by == core, w_mine_ref[:, first_beside], w_other_ref[:, first_beside]
        )
        w_both = jnp.concatenate([w_ref[:, pl.ds(first, columns)], w_beside], axis=0)
        out[...] = jnp.dot(both, w_both, preferred_element_type=jnp.float32).astype(out.dtype)


def project(place, own, beside, w_out, w_mine, w_other):
    outs = [shape(*own.shape)] * 4
    return pl.pallas_call(
        project_kernel,
        in_specs=[pl.BlockSpec(memory_space=pltpu.SMEM)] + [vmem()] * 5,
        out_specs=[vmem()] * len(outs),
        out_shape=outs,
        compiler_params=PARAMS,
        name="project",
    )(jnp.stack(place).astype(jnp.int32), own, beside, w_out, w_mine, w_other)


def total_kernel(*refs):
    parts, (value_ref, tangent_ref) = refs[:-2], refs[-2:]
    total = sum(part[...].astype(jnp.float32) for part in parts)
    rows = value_ref.shape[0]
    value_ref[...] = total[:rows].astype(value_ref.dtype)
    tangent_ref[...] = total[rows:].astype(tangent_ref.dtype)


SWAP = [(0, 1), (1, 0)]


def along_z(x, step):
    return lax.ppermute(x, "z", [(i, (i + step) % 8) for i in range(8)])


def beside(left, right):
    width = left.shape[1]
    low = jnp.array(-jnp.inf, left.dtype)
    return jnp.maximum(
        lax.pad(left, low, [(0, 0, 0), (0, width, 0)]),
        lax.pad(right, low, [(0, 0, 0), (width, 0, 0)]),
    )


def on_device(queries, keys, values, tan_queries, tan_keys, tan_values, w_out):
    rows, width = queries.shape
    own = [beside(keys, tan_keys), beside(values, tan_values)]
    def around(pair):
        return along_z(pair[0], 1), along_z(pair[1], -1)

    k_steps, v_steps = [(own[0], own[0])], [(own[1], own[1])]
    k_steps.append(around(k_steps[0]))
    v_steps.append(around(v_steps[0]))

    own_q = beside(tan_queries, queries)
    place = [lax.axis_index(name) for name in ("xl", "y", "core")]
    quarter = w_out.shape[1] // 4
    wanted = lax.dynamic_slice_in_dim(
        w_out, ((1 - place[0]) * 2 + place[2]) * quarter, quarter, axis=1
    )
    far_q = lax.ppermute(own_q, "xh", SWAP)
    stack = jnp.concatenate([own_q, far_q], axis=0)
    wanted, stack = lax.optimization_barrier((wanted, stack))
    stacks = [stack, lax.ppermute(stack, "core", SWAP)]

    k_steps.append(around(k_steps[1]))
    v_steps[1], k_steps[1] = lax.optimization_barrier((v_steps[1], k_steps[1]))
    v_steps.append(around(v_steps[1]))
    k_steps[2], v_steps[1] = lax.optimization_barrier((k_steps[2], v_steps[1]))
    k_steps.append(around(k_steps[2]))
    v_steps[2], k_steps[2], stacks = lax.optimization_barrier((v_steps[2], k_steps[2], stacks))
    v_steps.append(around(v_steps[2]))

    wanted, v_steps[1] = lax.optimization_barrier((wanted, v_steps[1]))
    w_mine = lax.ppermute(wanted, "xl", SWAP)

    def both_ways(step):
        return [x for pair in zip(k_steps[step], v_steps[step]) for x in pair]

    states = attend(stacks, own + both_ways(1))
    k_steps[3], v_steps[2], states = lax.optimization_barrier((k_steps[3], v_steps[2], states))
    last = [along_z(k_steps[3][0], 1)]
    states = attend(stacks, both_ways(2), states)
    v_steps[3], k_steps[3], states = lax.optimization_barrier((v_steps[3], k_steps[3], states))
    last.append(along_z(v_steps[3][1], -1))
    states = attend(stacks, both_ways(3), states)

    states, w_mine = lax.optimization_barrier((states, w_mine))
    other = attend(stacks[1:], last, states[1:], True)[0]
    other = lax.ppermute(other, "core", SWAP)
    mine = attend(stacks[:1], last, states[:1], True)[0]

    def join(first_row):
        def kernel(*refs):
            join_kernel(first_row, *refs)

        return call(kernel, "join", [shape(rows, mine.shape[1])], [mine, other])[0]

    from_far = lax.ppermute(join(rows), "xh", SWAP)
    near = join(0)
    attended = call(attended_kernel, "attended", [shape(2 * rows, width)], [near, from_far])[0]
    beside_attended = lax.ppermute(attended, "xl", SWAP)
    w_other = lax.ppermute(w_mine, "core", SWAP)
    parts = list(project(place, attended, beside_attended, w_out, w_mine, w_other))
    parts = parts[:1] + [
        lax.ppermute(part, "y", [(i, (i + step) % 4) for i in range(4)])
        for step, part in ((2, parts[2]), (1, parts[1]), (3, parts[3]))
    ]
    return tuple(call(total_kernel, "total", [shape(rows, width)] * 2, parts))


def solution(mesh):
    fine = Mesh(
        mesh.devices.reshape([size for _, size in CTX + HEAD]), [name for name, _ in CTX + HEAD]
    )
    ctx, head = tuple(name for name, _ in CTX), tuple(name for name, _ in HEAD)
    split = P(ctx, head)
    return jax.shard_map(
        on_device,
        mesh=fine,
        in_specs=(split,) * 6 + (P(head, None),),
        out_specs=(split, split),
        check_vma=False,
    )
```

```python
import math

import jax
import jax.numpy as jnp
from jax import lax
from jax.experimental import pallas as pl
from jax.experimental.pallas import tpu as pltpu
from jax.sharding import Mesh, PartitionSpec as P

DH = 128
FACTOR = 1.0 / math.sqrt(DH)
LOG2E = math.log2(math.e)
CTX = (("xh", 2), ("z", 8), ("core", 2))
HEAD = (("xl", 2), ("y", 4))
VMEM_LIMIT = 12 * 1024 * 1024
PARAMS = pltpu.CompilerParams(vmem_limit_bytes=VMEM_LIMIT)

_NT = (((1,), (1,)), ((), ()))


def vmem():
    return pl.BlockSpec(memory_space=pltpu.VMEM)


def call(kernel, name, outs, args, flops=0, transcendentals=0):
    moved = sum(x.size * x.dtype.itemsize for x in list(args) + list(outs))
    return pl.pallas_call(
        kernel,
        in_specs=[vmem()] * len(args),
        out_specs=[vmem()] * len(outs),
        out_shape=list(outs),
        compiler_params=PARAMS,
        cost_estimate=pl.CostEstimate(
            flops=flops, bytes_accessed=moved, transcendentals=transcendentals
        ),
        name=name,
    )(*args)


def shape(rows, columns, dtype=jnp.bfloat16):
    return jax.ShapeDtypeStruct((rows, columns), dtype)


def wide(column):
    return jnp.broadcast_to(column, (column.shape[0], DH))


def tiled(x, columns):
    whole = -(-columns // DH)
    return jnp.concatenate([x] * whole, axis=1)[:, :columns]


def stats_columns(logs, slopes):
    lane = lax.broadcasted_iota(jnp.int32, logs[0].shape, 1)
    stats = jnp.zeros(logs[0].shape, jnp.float32)
    third = jnp.zeros(logs[0].shape, jnp.int32)
    for at, value in enumerate(logs + slopes):
        stats = jnp.where(lane >= 3 * at, value, stats)
        third = jnp.where(lane >= 3 * at, 3 * at, third)
    third = lane - third
    high = stats.astype(jnp.bfloat16).astype(jnp.float32)
    rest = stats - high
    middle = rest.astype(jnp.bfloat16).astype(jnp.float32)
    kept = jnp.where(third == 0, high, jnp.where(third == 1, middle, rest - middle))
    return jnp.where(third < 3, kept, 0.0).astype(jnp.bfloat16)


def stats_of(part, heads):
    row = lax.broadcasted_iota(jnp.int32, (DH, 2 * heads * DH), 0)
    column = lax.broadcasted_iota(jnp.int32, (DH, 2 * heads * DH), 1)
    first = 3 * lax.shift_right_logical(column, DH.bit_length() - 1)
    chosen = ((row >= first) & (row < first + 3)).astype(jnp.bfloat16)
    sums = jnp.dot(part[:, 2 * heads * DH :], chosen, preferred_element_type=jnp.float32)
    columns = [sums[:, at * DH : (at + 1) * DH] for at in range(2 * heads)]
    return columns[:heads], columns[heads:]


def joined(parts, logs, slopes):
    top = logs[0]
    for log in logs[1:]:
        top = jnp.maximum(top, log)
    shares = [jnp.exp(log - top) for log in logs]
    total = sum(shares)
    inverse = 1.0 / total
    shares = [share * inverse for share in shares]
    mean_slope = sum(share * slope for share, slope in zip(shares, slopes))
    primal = sum(share * part[0] for share, part in zip(shares, parts))
    tangent = sum(
        share * (part[1] + (slope - mean_slope) * part[0])
        for share, slope, part in zip(shares, slopes, parts)
    )
    return primal, tangent, top + jnp.log(total), mean_slope


def head_of(part, head):
    both = part[:, 2 * head * DH : 2 * (head + 1) * DH].astype(jnp.float32)
    return both[:, :DH], both[:, DH:]


def attend_head(q_both, k_both, v_both, state):
    s = lax.dot_general(q_both[:, DH:], k_both[:, :DH], _NT, preferred_element_type=jnp.float32)
    slope = lax.dot_general(q_both, k_both, _NT, preferred_element_type=jnp.float32)
    peak = wide(jnp.max(s, axis=1, keepdims=True))
    if state is not None:
        peak = jnp.maximum(peak, state[2])
    weights = jnp.exp2((s - tiled(peak, s.shape[1])) * (FACTOR * LOG2E))
    total = wide(jnp.sum(weights, axis=1, keepdims=True))
    mixed = (weights * slope).astype(jnp.bfloat16)
    sums = jnp.dot(weights.astype(jnp.bfloat16), v_both, preferred_element_type=jnp.float32)
    value_one = jnp.concatenate([v_both[:, :DH], jnp.ones_like(v_both[:, :DH])], axis=1)
    more = jnp.dot(mixed, value_one, preferred_element_type=jnp.float32) * FACTOR
    primal, tangent, slope_total = sums[:, :DH], sums[:, DH:] + more[:, :DH], more[:, DH:]
    if state is not None:
        shrink = jnp.exp2((state[2] - peak) * (FACTOR * LOG2E))
        primal = primal + state[0] * shrink
        tangent = tangent + state[1] * shrink
        total = total + state[3] * shrink
        slope_total = slope_total + state[4] * shrink
    return primal, tangent, peak, total, slope_total


def attend_kernel(q_count, k_count, merge, final, *refs):
    q_refs, k_refs = refs[:q_count], refs[q_count : q_count + k_count]
    earlier = refs[q_count + k_count : 2 * q_count + k_count] if merge else ()
    outs = refs[-q_count:]
    heads = q_refs[0].shape[1] // (2 * DH)
    logs, slopes = [[] for _ in outs], [[] for _ in outs]

    def both(some, head):
        halves = [
            jnp.concatenate([ref[:, at * DH : (at + 1) * DH] for ref in some], axis=0)
            for at in (head, heads + head)
        ]
        return jnp.concatenate(halves, axis=1)

    for head in range(heads):
        k_both, v_both = both(k_refs[0::2], head), both(k_refs[1::2], head)
        for stack, out in enumerate(outs):
            state = None
            if merge:
                state = [
                    earlier[stack][:, (5 * head + at) * DH : (5 * head + at + 1) * DH]
                    for at in range(5)
                ]
            found = attend_head(both(q_refs[stack : stack + 1], head), k_both, v_both, state)
            if final:
                primal, tangent, peak, total, slope_total = found
                inverse = 1.0 / total
                mean_slope = slope_total * inverse
                primal = primal * inverse
                tangent = tangent * inverse - mean_slope * primal
                first = 2 * head * DH
                out[:, first : first + DH] = primal.astype(out.dtype)
                out[:, first + DH : first + 2 * DH] = tangent.astype(out.dtype)
                logs[stack].append(peak * FACTOR + jnp.log(total))
                slopes[stack].append(mean_slope)
            else:
                for at, x in enumerate(found):
                    out[:, (5 * head + at) * DH : (5 * head + at + 1) * DH] = x
    if final:
        for stack, out in enumerate(outs):
            out[:, 2 * heads * DH :] = stats_columns(logs[stack], slopes[stack])


def attend(q_stacks, k_blocks, earlier=None, final=False):
    rows, width = q_stacks[0].shape
    heads = width // (2 * DH)
    keys = sum(block.shape[0] for block in k_blocks) // 2
    merge = earlier is not None
    if final:
        outs = [shape(rows, (2 * heads + 1) * DH)] * len(q_stacks)
    else:
        outs = [shape(rows, 5 * heads * DH, jnp.float32)] * len(q_stacks)
    pairs = len(q_stacks) * rows * keys * heads

    def kernel(*refs):
        attend_kernel(len(q_stacks), len(k_blocks), merge, final, *refs)

    return call(
        kernel,
        "attend",
        outs,
        list(q_stacks) + list(k_blocks) + list(earlier or ()),
        flops=2 * pairs * DH * 8,
        transcendentals=pairs,
    )


def join_parts(parts):
    heads = (parts[0].shape[1] - DH) // (2 * DH)
    stats = [stats_of(part, heads) for part in parts]
    return [
        joined(
            [head_of(part, head) for part in parts],
            [stat[0][head] for stat in stats],
            [stat[1][head] for stat in stats],
        )
        for head in range(heads)
    ]


def join_kernel(first_row, a_ref, b_ref, out):
    own = pl.ds(first_row, out.shape[0])
    found = join_parts([a_ref[own, :], b_ref[own, :]])
    for head, (primal, tangent, _, _) in enumerate(found):
        first = 2 * head * DH
        out[:, first : first + DH] = primal.astype(out.dtype)
        out[:, first + DH : first + 2 * DH] = tangent.astype(out.dtype)
    out[:, 2 * len(found) * DH :] = stats_columns([f[2] for f in found], [f[3] for f in found])


def attended_kernel(a_ref, b_ref, out):
    found = join_parts([a_ref[...], b_ref[...]])
    rows = out.shape[0] // 2
    for head, each in enumerate(found):
        for at in range(2):
            out[at * rows : (at + 1) * rows, head * DH : (head + 1) * DH] = each[at].astype(out.dtype)


def project_own_kernel(at_ref, own_ref, w_ref, w_mine_ref, w_other_ref, *refs):
    xl, y, core = at_ref[0], at_ref[1], at_ref[2]
    count = len(refs) // 2
    columns = refs[0].shape[1]
    for step, (out, w_out_ref) in enumerate(zip(refs[:count], refs[count:])):
        target = lax.rem(y + step, count)
        first = pl.multiple_of((xl * count + target) * columns, DH)
        out[...] = jnp.dot(
            own_ref[...], w_ref[:, pl.ds(first, columns)], preferred_element_type=jnp.float32
        )
        fetched_by, place = lax.div(target, 2), lax.rem(target, 2)
        half = pl.ds(pl.multiple_of(place * columns, DH), columns)
        w_out_ref[...] = jnp.where(fetched_by == core, w_mine_ref[:, half], w_other_ref[:, half])


def project_kernel(beside_ref, *refs):
    count = len(refs) // 3
    for own, w_beside, out in zip(refs[:count], refs[count : 2 * count], refs[2 * count :]):
        total = own[...] + jnp.dot(
            beside_ref[...], w_beside[...], preferred_element_type=jnp.float32
        )
        out[...] = total.astype(out.dtype)


def project_own(where, own, w_out, w_mine, w_other):
    rows, columns = own.shape
    outs = [shape(rows, columns, jnp.float32)] * 4 + [shape(w_out.shape[0], columns)] * 4
    return pl.pallas_call(
        project_own_kernel,
        in_specs=[pl.BlockSpec(memory_space=pltpu.SMEM)] + [vmem()] * 4,
        out_specs=[vmem()] * len(outs),
        out_shape=outs,
        compiler_params=PARAMS,
        cost_estimate=pl.CostEstimate(
            flops=8 * rows * columns * columns,
            bytes_accessed=16 * rows * columns,
            transcendentals=0,
        ),
        name="project_own",
    )(where, own, w_out, w_mine, w_other)


def total_kernel(*refs):
    parts, (value_ref, tangent_ref) = refs[:-2], refs[-2:]
    total = sum(part[...].astype(jnp.float32) for part in parts)
    rows = value_ref.shape[0]
    value_ref[...] = total[:rows].astype(value_ref.dtype)
    tangent_ref[...] = total[rows:].astype(tangent_ref.dtype)


SWAP = [(0, 1), (1, 0)]


def along_z(x, step):
    return lax.ppermute(x, "z", [(i, (i + step) % 8) for i in range(8)])


def beside(left, right):
    width = left.shape[1]
    low = jnp.array(-jnp.inf, left.dtype)
    return jnp.maximum(
        lax.pad(left, low, [(0, 0, 0), (0, width, 0)]),
        lax.pad(right, low, [(0, 0, 0), (width, 0, 0)]),
    )


def on_device(queries, keys, values, tan_queries, tan_keys, tan_values, w_out):
    rows, width = queries.shape
    own = [beside(keys, tan_keys), beside(values, tan_values)]
    own_q = beside(tan_queries, queries)
    own_q, own[0] = lax.optimization_barrier((own_q, own[0]))
    def around(pair):
        return along_z(pair[0], 1), along_z(pair[1], -1)

    k_steps, v_steps = [(own[0], own[0])], [(own[1], own[1])]
    k_steps.append(around(k_steps[0]))
    v_steps.append(around(v_steps[0]))

    place = [lax.axis_index(name) for name in ("xl", "y", "core")]
    quarter = w_out.shape[1] // 4
    wanted = lax.dynamic_slice_in_dim(
        w_out, ((1 - place[0]) * 2 + place[2]) * quarter, quarter, axis=1
    )
    far_q = lax.ppermute(own_q, "xh", SWAP)
    stack = jnp.concatenate([own_q, far_q], axis=0)
    wanted, stack = lax.optimization_barrier((wanted, stack))
    stacks = [stack, lax.ppermute(stack, "core", SWAP)]

    k_steps.append(around(k_steps[1]))
    v_steps[1], k_steps[1] = lax.optimization_barrier((v_steps[1], k_steps[1]))
    v_steps.append(around(v_steps[1]))
    k_steps[2], v_steps[1] = lax.optimization_barrier((k_steps[2], v_steps[1]))
    k_steps.append(around(k_steps[2]))
    v_steps[2], k_steps[2], stacks = lax.optimization_barrier((v_steps[2], k_steps[2], stacks))
    v_steps.append(around(v_steps[2]))

    wanted, v_steps[1] = lax.optimization_barrier((wanted, v_steps[1]))
    w_mine = lax.ppermute(wanted, "xl", SWAP)

    def both_ways(step):
        return [x for pair in zip(k_steps[step], v_steps[step]) for x in pair]

    states = attend(stacks, own + both_ways(1))
    k_steps[3], v_steps[2], states = lax.optimization_barrier((k_steps[3], v_steps[2], states))
    last = [along_z(k_steps[3][0], 1)]
    states = attend(stacks, both_ways(2), states)
    v_steps[3], k_steps[3], states = lax.optimization_barrier((v_steps[3], k_steps[3], states))
    last.append(along_z(v_steps[3][1], -1))
    states = attend(stacks, both_ways(3), states)

    states, w_mine = lax.optimization_barrier((states, w_mine))
    other = attend(stacks[1:], last, states[1:], True)[0]
    other = lax.ppermute(other, "core", SWAP)
    mine = attend(stacks[:1], last, states[:1], True)[0]

    def join(first_row):
        def kernel(*refs):
            join_kernel(first_row, *refs)

        return call(kernel, "join", [shape(rows, mine.shape[1])], [mine, other])[0]

    from_far = lax.ppermute(join(rows), "xh", SWAP)
    near = join(0)
    attended = call(attended_kernel, "attended", [shape(2 * rows, width)], [near, from_far])[0]
    beside_attended = lax.ppermute(attended, "xl", SWAP)
    w_other = lax.ppermute(w_mine, "core", SWAP)
    where = jnp.stack(place).astype(jnp.int32)
    ready = project_own(where, attended, w_out, w_mine, w_other)
    parts = call(
        project_kernel,
        "project",
        [shape(*attended.shape)] * 4,
        [beside_attended] + list(ready),
        flops=8 * 2 * rows * width * width,
    )
    parts = list(parts)
    parts = parts[:1] + [
        lax.ppermute(part, "y", [(i, (i + step) % 4) for i in range(4)])
        for step, part in ((2, parts[2]), (1, parts[1]), (3, parts[3]))
    ]
    return tuple(call(total_kernel, "total", [shape(rows, width)] * 2, parts))


def solution(mesh):
    fine = Mesh(
        mesh.devices.reshape([size for _, size in CTX + HEAD]), [name for name, _ in CTX + HEAD]
    )
    ctx, head = tuple(name for name, _ in CTX), tuple(name for name, _ in HEAD)
    split = P(ctx, head)
    return jax.shard_map(
        on_device,
        mesh=fine,
        in_specs=(split,) * 6 + (P(head, None),),
        out_specs=(split, split),
        check_vma=False,
    )
```

```python
import math

import jax
import jax.numpy as jnp
from jax import lax
from jax.experimental import pallas as pl
from jax.experimental.pallas import tpu as pltpu
from jax.sharding import Mesh, PartitionSpec as P

DH = 128
FACTOR = 1.0 / math.sqrt(DH)
LOG2E = math.log2(math.e)
CTX = (("xh", 2), ("z", 8), ("core", 2))
HEAD = (("xl", 2), ("y", 4))
VMEM_LIMIT = 12 * 1024 * 1024
PARAMS = pltpu.CompilerParams(vmem_limit_bytes=VMEM_LIMIT)

_NT = (((1,), (1,)), ((), ()))


def vmem():
    return pl.BlockSpec(memory_space=pltpu.VMEM)


def call(kernel, name, outs, args, flops=0, transcendentals=0):
    moved = sum(x.size * x.dtype.itemsize for x in list(args) + list(outs))
    return pl.pallas_call(
        kernel,
        in_specs=[vmem()] * len(args),
        out_specs=[vmem()] * len(outs),
        out_shape=list(outs),
        compiler_params=PARAMS,
        cost_estimate=pl.CostEstimate(
            flops=flops, bytes_accessed=moved, transcendentals=transcendentals
        ),
        name=name,
    )(*args)


def shape(rows, columns, dtype=jnp.bfloat16):
    return jax.ShapeDtypeStruct((rows, columns), dtype)


def wide(column):
    return jnp.broadcast_to(column, (column.shape[0], DH))


def tiled(x, columns):
    whole = -(-columns // DH)
    return jnp.concatenate([x] * whole, axis=1)[:, :columns]


def stats_columns(logs, slopes):
    lane = lax.broadcasted_iota(jnp.int32, logs[0].shape, 1)
    stats = jnp.zeros(logs[0].shape, jnp.float32)
    third = jnp.zeros(logs[0].shape, jnp.int32)
    for at, value in enumerate(logs + slopes):
        stats = jnp.where(lane >= 3 * at, value, stats)
        third = jnp.where(lane >= 3 * at, 3 * at, third)
    third = lane - third
    high = stats.astype(jnp.bfloat16).astype(jnp.float32)
    rest = stats - high
    middle = rest.astype(jnp.bfloat16).astype(jnp.float32)
    kept = jnp.where(third == 0, high, jnp.where(third == 1, middle, rest - middle))
    return jnp.where(third < 3, kept, 0.0).astype(jnp.bfloat16)


def stats_of(part, heads):
    row = lax.broadcasted_iota(jnp.int32, (DH, 2 * heads * DH), 0)
    column = lax.broadcasted_iota(jnp.int32, (DH, 2 * heads * DH), 1)
    first = 3 * lax.shift_right_logical(column, DH.bit_length() - 1)
    chosen = ((row >= first) & (row < first + 3)).astype(jnp.bfloat16)
    sums = jnp.dot(part[:, 2 * heads * DH :], chosen, preferred_element_type=jnp.float32)
    columns = [sums[:, at * DH : (at + 1) * DH] for at in range(2 * heads)]
    return columns[:heads], columns[heads:]


def joined(parts, logs, slopes):
    top = logs[0]
    for log in logs[1:]:
        top = jnp.maximum(top, log)
    shares = [jnp.exp(log - top) for log in logs]
    total = sum(shares)
    inverse = 1.0 / total
    shares = [share * inverse for share in shares]
    mean_slope = sum(share * slope for share, slope in zip(shares, slopes))
    primal = sum(share * part[0] for share, part in zip(shares, parts))
    tangent = sum(
        share * (part[1] + (slope - mean_slope) * part[0])
        for share, slope, part in zip(shares, slopes, parts)
    )
    return primal, tangent, top + jnp.log(total), mean_slope


def head_of(part, head):
    both = part[:, 2 * head * DH : 2 * (head + 1) * DH].astype(jnp.float32)
    return both[:, :DH], both[:, DH:]


def attend_head(q_both, k_both, v_both, state):
    s = lax.dot_general(q_both[:, DH:], k_both[:, :DH], _NT, preferred_element_type=jnp.float32)
    slope = lax.dot_general(q_both, k_both, _NT, preferred_element_type=jnp.float32)
    peak = wide(jnp.max(s, axis=1, keepdims=True))
    if state is not None:
        peak = jnp.maximum(peak, state[2])
    weights = jnp.exp2((s - tiled(peak, s.shape[1])) * (FACTOR * LOG2E))
    total = wide(jnp.sum(weights, axis=1, keepdims=True))
    mixed = (weights * slope).astype(jnp.bfloat16)
    sums = jnp.dot(weights.astype(jnp.bfloat16), v_both, preferred_element_type=jnp.float32)
    value_one = jnp.concatenate([v_both[:, :DH], jnp.ones_like(v_both[:, :DH])], axis=1)
    more = jnp.dot(mixed, value_one, preferred_element_type=jnp.float32) * FACTOR
    primal, tangent, slope_total = sums[:, :DH], sums[:, DH:] + more[:, :DH], more[:, DH:]
    if state is not None:
        shrink = jnp.exp2((state[2] - peak) * (FACTOR * LOG2E))
        primal = primal + state[0] * shrink
        tangent = tangent + state[1] * shrink
        total = total + state[3] * shrink
        slope_total = slope_total + state[4] * shrink
    return primal, tangent, peak, total, slope_total


def attend_kernel(q_count, k_count, merge, final, *refs):
    q_refs, k_refs = refs[:q_count], refs[q_count : q_count + k_count]
    earlier = refs[q_count + k_count : 2 * q_count + k_count] if merge else ()
    outs = refs[-q_count:]
    heads = q_refs[0].shape[1] // (2 * DH)
    logs, slopes = [[] for _ in outs], [[] for _ in outs]

    def both(some, head):
        halves = [
            jnp.concatenate([ref[:, at * DH : (at + 1) * DH] for ref in some], axis=0)
            for at in (head, heads + head)
        ]
        return jnp.concatenate(halves, axis=1)

    for head in range(heads):
        k_both, v_both = both(k_refs[0::2], head), both(k_refs[1::2], head)
        for stack, out in enumerate(outs):
            state = None
            if merge:
                state = [
                    earlier[stack][:, (5 * head + at) * DH : (5 * head + at + 1) * DH]
                    for at in range(5)
                ]
            found = attend_head(both(q_refs[stack : stack + 1], head), k_both, v_both, state)
            if final:
                primal, tangent, peak, total, slope_total = found
                inverse = 1.0 / total
                mean_slope = slope_total * inverse
                primal = primal * inverse
                tangent = tangent * inverse - mean_slope * primal
                first = 2 * head * DH
                out[:, first : first + DH] = primal.astype(out.dtype)
                out[:, first + DH : first + 2 * DH] = tangent.astype(out.dtype)
                logs[stack].append(peak * FACTOR + jnp.log(total))
                slopes[stack].append(mean_slope)
            else:
                for at, x in enumerate(found):
                    out[:, (5 * head + at) * DH : (5 * head + at + 1) * DH] = x
    if final:
        for stack, out in enumerate(outs):
            out[:, 2 * heads * DH :] = stats_columns(logs[stack], slopes[stack])


def attend(q_stacks, k_blocks, earlier=None, final=False):
    rows, width = q_stacks[0].shape
    heads = width // (2 * DH)
    keys = sum(block.shape[0] for block in k_blocks) // 2
    merge = earlier is not None
    if final:
        outs = [shape(rows, (2 * heads + 1) * DH)] * len(q_stacks)
    else:
        outs = [shape(rows, 5 * heads * DH, jnp.float32)] * len(q_stacks)
    pairs = len(q_stacks) * rows * keys * heads

    def kernel(*refs):
        attend_kernel(len(q_stacks), len(k_blocks), merge, final, *refs)

    return call(
        kernel,
        "attend",
        outs,
        list(q_stacks) + list(k_blocks) + list(earlier or ()),
        flops=2 * pairs * DH * 8,
        transcendentals=pairs,
    )


def join_parts(parts):
    heads = (parts[0].shape[1] - DH) // (2 * DH)
    stats = [stats_of(part, heads) for part in parts]
    return [
        joined(
            [head_of(part, head) for part in parts],
            [stat[0][head] for stat in stats],
            [stat[1][head] for stat in stats],
        )
        for head in range(heads)
    ]


def join_kernel(first_row, a_ref, b_ref, out):
    own = pl.ds(first_row, out.shape[0])
    found = join_parts([a_ref[own, :], b_ref[own, :]])
    for head, (primal, tangent, _, _) in enumerate(found):
        first = 2 * head * DH
        out[:, first : first + DH] = primal.astype(out.dtype)
        out[:, first + DH : first + 2 * DH] = tangent.astype(out.dtype)
    out[:, 2 * len(found) * DH :] = stats_columns([f[2] for f in found], [f[3] for f in found])


def attended_kernel(a_ref, b_ref, out):
    found = join_parts([a_ref[...], b_ref[...]])
    rows = out.shape[0] // 2
    for head, each in enumerate(found):
        for at in range(2):
            out[at * rows : (at + 1) * rows, head * DH : (head + 1) * DH] = each[at].astype(out.dtype)


def project_own_kernel(at_ref, own_ref, w_ref, w_mine_ref, w_other_ref, *refs):
    xl, y, core = at_ref[0], at_ref[1], at_ref[2]
    count = len(refs) // 2
    columns = refs[0].shape[1]
    for step, (out, w_out_ref) in enumerate(zip(refs[:count], refs[count:])):
        target = lax.rem(y + step, count)
        first = pl.multiple_of((xl * count + target) * columns, DH)
        out[...] = jnp.dot(
            own_ref[...], w_ref[:, pl.ds(first, columns)], preferred_element_type=jnp.float32
        )
        fetched_by, place = lax.div(target, 2), lax.rem(target, 2)
        half = pl.ds(pl.multiple_of(place * columns, DH), columns)
        w_out_ref[...] = jnp.where(fetched_by == core, w_mine_ref[:, half], w_other_ref[:, half])


def project_kernel(beside_ref, *refs):
    count = len(refs) // 3
    for own, w_beside, out in zip(refs[:count], refs[count : 2 * count], refs[2 * count :]):
        total = own[...] + jnp.dot(
            beside_ref[...], w_beside[...], preferred_element_type=jnp.float32
        )
        out[...] = total.astype(out.dtype)


def project_own(where, own, w_out, w_mine, w_other):
    rows, columns = own.shape
    outs = [shape(rows, columns, jnp.float32)] * 4 + [shape(w_out.shape[0], columns)] * 4
    return pl.pallas_call(
        project_own_kernel,
        in_specs=[pl.BlockSpec(memory_space=pltpu.SMEM)] + [vmem()] * 4,
        out_specs=[vmem()] * len(outs),
        out_shape=outs,
        compiler_params=PARAMS,
        cost_estimate=pl.CostEstimate(
            flops=8 * rows * columns * columns,
            bytes_accessed=16 * rows * columns,
            transcendentals=0,
        ),
        name="project_own",
    )(where, own, w_out, w_mine, w_other)


def early_kernel(a_ref, b_ref, out):
    out[...] = a_ref[...].astype(jnp.float32) + b_ref[...].astype(jnp.float32)


def total_kernel(*refs):
    parts, (value_ref, tangent_ref) = refs[:-2], refs[-2:]
    total = sum(part[...].astype(jnp.float32) for part in parts)
    rows = value_ref.shape[0]
    value_ref[...] = total[:rows].astype(value_ref.dtype)
    tangent_ref[...] = total[rows:].astype(tangent_ref.dtype)


SWAP = [(0, 1), (1, 0)]


def along_z(x, step):
    return lax.ppermute(x, "z", [(i, (i + step) % 8) for i in range(8)])


def beside(left, right):
    width = left.shape[1]
    low = jnp.array(-jnp.inf, left.dtype)
    return jnp.maximum(
        lax.pad(left, low, [(0, 0, 0), (0, width, 0)]),
        lax.pad(right, low, [(0, 0, 0), (width, 0, 0)]),
    )


def on_device(queries, keys, values, tan_queries, tan_keys, tan_values, w_out):
    rows, width = queries.shape
    own = [beside(keys, tan_keys), beside(values, tan_values)]
    own_q = beside(tan_queries, queries)
    own_q, own[0] = lax.optimization_barrier((own_q, own[0]))
    def around(pair):
        return along_z(pair[0], 1), along_z(pair[1], -1)

    k_steps, v_steps = [(own[0], own[0])], [(own[1], own[1])]
    k_steps.append(around(k_steps[0]))
    v_steps.append(around(v_steps[0]))

    place = [lax.axis_index(name) for name in ("xl", "y", "core")]
    quarter = w_out.shape[1] // 4
    wanted = lax.dynamic_slice_in_dim(
        w_out, ((1 - place[0]) * 2 + place[2]) * quarter, quarter, axis=1
    )
    far_q = lax.ppermute(own_q, "xh", SWAP)
    stack = jnp.concatenate([own_q, far_q], axis=0)
    wanted, stack = lax.optimization_barrier((wanted, stack))
    stacks = [stack, lax.ppermute(stack, "core", SWAP)]

    k_steps.append(around(k_steps[1]))
    v_steps[1], k_steps[1] = lax.optimization_barrier((v_steps[1], k_steps[1]))
    v_steps.append(around(v_steps[1]))
    k_steps[2], v_steps[1] = lax.optimization_barrier((k_steps[2], v_steps[1]))
    k_steps.append(around(k_steps[2]))
    v_steps[2], k_steps[2], stacks = lax.optimization_barrier((v_steps[2], k_steps[2], stacks))
    v_steps.append(around(v_steps[2]))

    wanted, v_steps[1] = lax.optimization_barrier((wanted, v_steps[1]))
    w_mine = lax.ppermute(wanted, "xl", SWAP)

    def both_ways(step):
        return [x for pair in zip(k_steps[step], v_steps[step]) for x in pair]

    states = attend(stacks, own + both_ways(1))
    k_steps[3], v_steps[2], states = lax.optimization_barrier((k_steps[3], v_steps[2], states))
    last = [along_z(k_steps[3][0], 1)]
    states = attend(stacks, both_ways(2), states)
    v_steps[3], k_steps[3], states = lax.optimization_barrier((v_steps[3], k_steps[3], states))
    last.append(along_z(v_steps[3][1], -1))
    states = attend(stacks, both_ways(3), states)

    states, w_mine = lax.optimization_barrier((states, w_mine))
    other = attend(stacks[1:], last, states[1:], True)[0]
    other = lax.ppermute(other, "core", SWAP)
    mine = attend(stacks[:1], last, states[:1], True)[0]

    def join(first_row):
        def kernel(*refs):
            join_kernel(first_row, *refs)

        return call(kernel, "join", [shape(rows, mine.shape[1])], [mine, other])[0]

    from_far = lax.ppermute(join(rows), "xh", SWAP)
    near = join(0)
    attended = call(attended_kernel, "attended", [shape(2 * rows, width)], [near, from_far])[0]
    beside_attended = lax.ppermute(attended, "xl", SWAP)
    w_other = lax.ppermute(w_mine, "core", SWAP)
    where = jnp.stack(place).astype(jnp.int32)
    ready = project_own(where, attended, w_out, w_mine, w_other)
    parts = call(
        project_kernel,
        "project",
        [shape(*attended.shape)] * 4,
        [beside_attended] + list(ready),
        flops=8 * 2 * rows * width * width,
    )
    parts = list(parts)
    parts = parts[:1] + [
        lax.ppermute(part, "y", [(i, (i + step) % 4) for i in range(4)])
        for step, part in ((2, parts[2]), (1, parts[1]), (3, parts[3]))
    ]
    early = call(early_kernel, "early", [shape(2 * rows, width, jnp.float32)], parts[:2])
    return tuple(call(total_kernel, "total", [shape(rows, width)] * 2, list(early) + parts[2:]))


def solution(mesh):
    fine = Mesh(
        mesh.devices.reshape([size for _, size in CTX + HEAD]), [name for name, _ in CTX + HEAD]
    )
    ctx, head = tuple(name for name, _ in CTX), tuple(name for name, _ in HEAD)
    split = P(ctx, head)
    return jax.shard_map(
        on_device,
        mesh=fine,
        in_specs=(split,) * 6 + (P(head, None),),
        out_specs=(split, split),
        check_vma=False,
    )
```
